32 devices in a mesh: nodes: 8 (over z, x), heads: 4 (over y, core).
Axes of the slice: x: 2, y: 2, z: 4, core: 2. Of those that a mesh axis runs over, the one named last changes fastest.
Arguments:
- tokens: bfloat16 [8192, 512], P(('nodes', 'heads')), may hold values from -6 to 6
- w_qkv: bfloat16 [512, 1536], replicated, may hold values from -0.25 to 0.25
- w_out: bfloat16 [512, 512], replicated, may hold values from -0.5 to 0.5
- w_up: bfloat16 [512, 1024], replicated, may hold values from -0.25 to 0.25
- w_down: bfloat16 [1024, 512], replicated, may hold values from -0.1875 to 0.1875
- tile_cols: int32 [64, 8], P('nodes'), may hold values from 0 to 67, as said below
- tile_mask: int32 [64, 8, 128, 128], P('nodes'), may hold values from 0 to 1, as said below
- hub_blocks: int32 [4], replicated, may hold values from 0 to 63, as said below
Outputs:
- layer_out: bfloat16 [8192, 512], P(('nodes', 'heads'))
The draws below stay inside these ranges and needn't reach their ends.
Inputs may be any that keep to these rules, and one draw needn't show every extreme that they name: `tile_cols`: row block b belongs to node group b // 8. Tile 0 of b is b itself; tile 1 lies in the group before (cyclically over 8 groups), tile 2 in the group after, tile 3 is a hub slot; every other entry lies in those three groups or is a hub slot. Padding tiles have column b. `tile_mask`: the diagonal of tile 0 is all ones; tiles 0 to 3 are never padding, and padding tiles are all zero. `hub_blocks`: distinct blocks; the first and the last block are always among them.
All inputs are finite; a program needn't handle non-finite values.
Results may differ from the reference program's by a relative error of at most 0.0055.
Values may be sent and summed in bfloat16 or wider, within the bound.
No kernel may reach another device: no remote copies, remote signals or barrier semaphores. Data moves between devices by JAX's collectives and lax.ppermute only.
A program may use at most 64 MiB of HBM per device.

```python
import jax
import jax.numpy as jnp
from jax import lax

D = 512
FF = 1024
HEADS = 4
TB = 128
TILES = 8
HUBS = 4
GB = 8
BLOCKS = 64
NODES = 8192


def tile_plan(key):
    key_rows = jax.random.split(key, 7)
    others = (1 + jax.random.permutation(key_rows[0], BLOCKS - 2)[:HUBS - 2]).astype(jnp.int32)
    ordered = jnp.concatenate([jnp.zeros((1,), jnp.int32), others, jnp.full((1,), BLOCKS - 1, jnp.int32)])
    hubs = ordered[jax.random.permutation(key_rows[6], HUBS)].astype(jnp.int32)
    groups = BLOCKS // GB
    rows = jnp.arange(BLOCKS, dtype=jnp.int32)
    group = rows // GB
    before = (group - 1) % groups * GB + jax.random.randint(key_rows[1], (BLOCKS,), 0, GB)
    after = (group + 1) % groups * GB + jax.random.randint(key_rows[2], (BLOCKS,), 0, GB)
    shift_value = jax.random.randint(key_rows[3], (), 0, HUBS)
    first_hub = BLOCKS + (rows + shift_value) % HUBS
    pick = jax.random.randint(key_rows[4], (BLOCKS, TILES - 4), 0, 3 * GB + HUBS)
    near = (group[:, None] - 1 + pick // GB) % groups * GB + pick % GB
    far = BLOCKS + jnp.clip(pick - 3 * GB, 0, HUBS - 1)
    extra = jnp.where(pick < 3 * GB, near, far)
    cols = jnp.concatenate([rows[:, None], before[:, None], after[:, None], first_hub[:, None], extra], axis=1)
    live = jax.random.randint(key_rows[5], (BLOCKS,), 4, TILES + 1)
    slots = jnp.arange(TILES, dtype=jnp.int32)[None, :]
    cols = jnp.where(slots < live[:, None], cols, rows[:, None]).astype(jnp.int32)
    return (hubs, cols, live)


def draw_tile_cols(key, part):
    hubs, cols, live = tile_plan(key)
    return cols


def draw_hub_blocks(key, part):
    hubs, cols, live = tile_plan(key)
    return hubs


def draw_tile_mask(key, part):
    hubs, cols, live = tile_plan(key)
    key = jax.random.fold_in(key, 7)
    first, second = jax.random.split(key)
    density = jax.random.randint(first, (BLOCKS, 1, 1, 1), 2, 17)
    coins = jax.random.randint(second, (BLOCKS, TILES, TB, TB), 0, 32)
    edges = (coins < density).astype(jnp.int32)
    diagonal = jnp.eye(TB, dtype=jnp.int32)[None, None]
    first_tile = (jnp.arange(TILES) == 0).astype(jnp.int32)[None, :, None, None]
    edges = jnp.maximum(edges, diagonal * first_tile)
    used = (jnp.arange(TILES)[None, :] < live[:, None]).astype(jnp.int32)[:, :, None, None]
    return (edges * used).astype(jnp.int32)


def shard_levels(stream_key, shape, cuts, smallest, high):
    loudness, own = 1.0, jax.random.fold_in(stream_key, 6)
    for dim, blocks in cuts:
        heights = jnp.exp(jax.random.uniform(jax.random.fold_in(own, dim), (blocks,), jnp.float32, smallest / len(cuts), high / len(cuts)))
        loudness = loudness * jnp.repeat(heights, shape[dim] // blocks).reshape([-1 if axis == dim else 1 for axis in range(len(shape))])
    return loudness


def centred(rng, dims, scale, most, cuts=(), held_as=jnp.bfloat16):
    level = shard_levels(rng, dims, cuts, -0.22, 0.18) if cuts else 1.0
    entries = jax.random.normal(rng, dims, jnp.float32) * scale * level
    return jnp.minimum(jnp.maximum(entries, -most), most).astype(held_as)


def setup_inputs(seed: int = 0) -> dict:
    streams_of = jax.random.split(jax.random.key(seed), 9)
    tokens = centred(streams_of[0], (NODES, D), 1.0, 6.0, ((0, 32),))
    w_qkv = centred(streams_of[1], (D, 3 * D), D ** -0.5, 0.25)
    w_out = centred(streams_of[2], (D, D), (D // 4) ** -0.5, 0.5)
    w_up = centred(streams_of[3], (D, FF), D ** -0.5, 0.25)
    w_down = centred(streams_of[4], (FF, D), FF ** -0.5, 0.1875)
    tile_cols = draw_tile_cols(jax.random.fold_in(streams_of[8], 71), 0)
    tile_mask = draw_tile_mask(jax.random.fold_in(streams_of[8], 71), 0)
    hub_blocks = draw_hub_blocks(jax.random.fold_in(streams_of[8], 71), 0)
    return {"tokens": tokens, "w_qkv": w_qkv, "w_out": w_out, "w_up": w_up, "w_down": w_down, "tile_cols": tile_cols, "tile_mask": tile_mask, "hub_blocks": hub_blocks}


def layer_norm(value_rows):
    mean = lax.optimization_barrier(jnp.mean(value_rows, axis=-1, keepdims=True))
    centered = value_rows - mean
    spread = lax.optimization_barrier(jnp.mean(centered * centered, axis=-1, keepdims=True))
    return centered * lax.rsqrt(spread + 1e-05)

def reference(tokens, w_qkv, w_out, w_up, w_down, tile_cols, tile_mask, hub_blocks):
    head_dim = D // HEADS
    scale = 1.0 / head_dim ** 0.5
    features = tokens.astype(jnp.float32)
    normed = layer_norm(features).astype(jnp.bfloat16)
    qkv = jnp.dot(normed, w_qkv, preferred_element_type=jnp.float32).astype(jnp.bfloat16)
    qkv = qkv.reshape(BLOCKS, TB, HEADS, 3, head_dim)
    queries = qkv[:, :, :, 0, :]
    keyval = qkv[:, :, :, 1:, :]
    hub_index = jnp.clip(tile_cols - BLOCKS, 0, HUBS - 1).astype(jnp.int32)
    resolved = jnp.where(tile_cols >= BLOCKS, hub_blocks[hub_index], tile_cols).astype(jnp.int32)

    def one_block(inputs):
        block_cols, block_mask, query_block_rows = inputs
        gathered = keyval[block_cols]
        key_rows = gathered[:, :, :, 0, :].astype(jnp.float32)
        value_rows = gathered[:, :, :, 1, :].astype(jnp.float32)
        score_matrix = jnp.einsum('qhd,tkhd->htqk', query_block_rows.astype(jnp.float32), key_rows)
        weight = jnp.exp(score_matrix * scale) * block_mask.astype(jnp.float32)[None]
        total = lax.optimization_barrier(jnp.sum(weight, axis=(1, 3)))
        rounded_state = lax.optimization_barrier(weight.astype(jnp.bfloat16)).astype(jnp.float32)
        summed_state = jnp.einsum('htqk,tkhd->qhd', rounded_state, value_rows)
        return (summed_state / jnp.transpose(total)[:, :, None]).astype(jnp.bfloat16)
    attn = lax.map(one_block, (resolved, tile_mask, queries)).reshape(NODES, D)
    mid = features + jnp.dot(attn, w_out, preferred_element_type=jnp.float32)
    second_normed_state = layer_norm(mid).astype(jnp.bfloat16)
    hidden = jax.nn.gelu(jnp.dot(second_normed_state, w_up, preferred_element_type=jnp.float32), approximate=False).astype(jnp.bfloat16)
    return (mid + jnp.dot(hidden, w_down, preferred_element_type=jnp.float32)).astype(jnp.bfloat16)
```

```python
import functools

import jax
import jax.numpy as jnp
from jax import lax
from jax.experimental import pallas as pl
from jax.experimental.pallas import tpu as pltpu
from jax.sharding import PartitionSpec as P

TB = 128
PIECES = 8
PIECE = TB // PIECES
AXES = ("nodes", "heads")
ANY = pl.BlockSpec(memory_space=pl.ANY)
VMEM = pl.BlockSpec(memory_space=pltpu.VMEM)


def send(value, nodes, heads, where):
    pairs = []
    for n in range(nodes):
        for h in range(heads):
            to_n, to_h = where(n, h)
            pairs.append((n * heads + h, to_n % nodes * heads + to_h))
    return lax.ppermute(value, AXES, pairs)


def layer_norm(value_rows):
    mean = jnp.mean(value_rows, axis=-1, keepdims=True)
    centered = value_rows - mean
    spread = jnp.mean(centered * centered, axis=-1, keepdims=True)
    return (centered * lax.rsqrt(spread + 1e-05)).astype(jnp.bfloat16)


def project(normed, w_ref, cols):
    return jnp.dot(normed, w_ref[:, cols], preferred_element_type=jnp.float32).astype(
        jnp.bfloat16
    )


def keyval_into(out_ref, rows, normed, w_ref, heads, head_dim):
    width = heads * head_dim
    if head_dim % 128 == 0:
        for h in range(heads):
            both = project(normed, w_ref, slice((3 * h + 1) * head_dim, (3 * h + 3) * head_dim))
            out_ref[rows, h * head_dim : (h + 1) * head_dim] = both[:, :head_dim]
            out_ref[rows, width + h * head_dim : width + (h + 1) * head_dim] = both[:, head_dim:]
    else:
        out_ref[rows, :] = project(normed, w_ref, slice(width, 3 * width))


def query_into(out_ref, normed, w_ref, heads, head_dim):
    if head_dim % 128 == 0:
        for h in range(heads):
            out_ref[:, h * head_dim : (h + 1) * head_dim] = project(
                normed, w_ref, slice(3 * h * head_dim, (3 * h + 1) * head_dim)
            )
    else:
        out_ref[...] = project(normed, w_ref, slice(0, heads * head_dim))


def keyval_kernel(heads, head_dim, first_ref, second_ref, w_ref, out_ref, *query_ref):
    node_dev = first_ref.shape[0]
    for at, ref in enumerate((first_ref, second_ref)):
        normed = layer_norm(ref[...].astype(jnp.float32))
        keyval_into(out_ref, slice(at * node_dev, (at + 1) * node_dev), normed, w_ref, heads, head_dim)
        if at == 0 and query_ref:
            query_into(query_ref[0], normed, w_ref, heads, head_dim)


def keyvals(first, second, w_qkv, heads, head_dim, with_query):
    node_dev, width = first.shape
    out_shape = [jax.ShapeDtypeStruct((2 * node_dev, 2 * width), jnp.bfloat16)]
    if with_query:
        out_shape.append(jax.ShapeDtypeStruct((node_dev, width), jnp.bfloat16))
    return pl.pallas_call(
        functools.partial(keyval_kernel, heads, head_dim),
        out_shape=out_shape,
        in_specs=[VMEM] * 3,
        out_specs=[VMEM] * len(out_shape),
        compiler_params=pltpu.CompilerParams(vmem_limit_bytes=16 << 20),
        cost_estimate=pl.CostEstimate(
            flops=8 * node_dev * width * width, bytes_accessed=6 * width * width, transcendentals=0
        ),
        name="keyvals",
    )(first, second, w_qkv)


def pick_kernel(hub_count, plan_ref, *refs):
    sources, out_ref, sem = refs[:8], refs[8], refs[9]
    for j in range(hub_count):
        code, slot = plan_ref[2 * j], plan_ref[2 * j + 1]
        place = out_ref.at[j * PIECE : (j + 1) * PIECE]
        for k, ref in enumerate(sources):
            @pl.when(code == k)
            def _():
                if k < 6:
                    row = slot * TB + plan_ref[2 * hub_count] * PIECE
                else:
                    row = slot * 2 * PIECE + plan_ref[2 * hub_count + 1] * PIECE
                rows = pl.ds(pl.multiple_of(row, PIECE), PIECE)
                pltpu.make_async_copy(ref.at[rows], place, sem.at[j]).start()

        @pl.when(code >= 8)
        def _():
            out_ref[j * PIECE : (j + 1) * PIECE] = jnp.zeros((PIECE, out_ref.shape[1]), out_ref.dtype)

    for j in range(hub_count):
        @pl.when(plan_ref[2 * j] < 8)
        def _():
            place = out_ref.at[j * PIECE : (j + 1) * PIECE]
            pltpu.make_async_copy(sources[0].at[0:PIECE], place, sem.at[j]).wait()


def pick_pieces(plan, sources, hub_count):
    width = sources[0].shape[1]
    return pl.pallas_call(
        functools.partial(pick_kernel, hub_count),
        out_shape=jax.ShapeDtypeStruct((hub_count * PIECE, width), jnp.bfloat16),
        in_specs=[pl.BlockSpec(memory_space=pltpu.SMEM)] + [ANY] * 8,
        out_specs=VMEM,
        scratch_shapes=[pltpu.SemaphoreType.DMA((hub_count,))],
        name="pick_pieces",
    )(plan, *sources)


def final_kernel(
    heads, head_dim, hub_count, tiles, count,
    plan_ref, tokens_ref, query_ref, hub_a_ref, hub_b_ref, mask_ref, w_qkv_ref, w_out_ref, w_up_ref, w_down_ref, *refs
):
    stores, out_ref = refs[:count], refs[count]
    tile_ref, hub_kv, hub_rows, mask, w_qkv, w_out, w_up, w_down, attn, tile_sem, sem = refs[count + 1 :]
    node_dev, width = tokens_ref.shape
    local = node_dev // TB
    slots = local * tiles
    in_store = stores[0].shape[0] // TB
    loads = [
        pltpu.make_async_copy(w_qkv_ref, w_qkv, sem.at[0]),
        pltpu.make_async_copy(
            mask_ref.at[pl.ds(plan_ref[slots] * local, local)], mask, sem.at[1]
        ),
        pltpu.make_async_copy(w_out_ref, w_out, sem.at[2]),
        pltpu.make_async_copy(w_up_ref, w_up, sem.at[3]),
        pltpu.make_async_copy(w_down_ref, w_down, sem.at[4]),
    ]
    loads[0].start()
    for i in range(slots):
        index = plan_ref[i]
        for a, store in enumerate(stores):
            @pl.when(index // in_store == a)
            def _():
                rows = pl.ds(pl.multiple_of(index % in_store * TB, TB), TB)
                pltpu.make_async_copy(store.at[rows], tile_ref.at[i], tile_sem.at[i]).start()

    for load in loads[1:]:
        load.start()
    half = PIECES // 2
    for k in range(PIECES):
        source = hub_b_ref if k & 1 else hub_a_ref
        piece = plan_ref[slots + 1 + k]
        for j in range(hub_count):
            row = (k >> 1) * hub_count * PIECE + j * PIECE
            place = pl.ds(pl.multiple_of(j * TB + piece * PIECE, PIECE), PIECE)
            hub_rows[place, :] = source[row : row + PIECE, :]
    hub_normed = layer_norm(hub_rows[...].astype(jnp.float32))
    loads[0].wait()
    keyval_into(hub_kv, slice(None), hub_normed, w_qkv, heads, head_dim)
    hub_base = count * in_store
    for i in range(slots):
        index = plan_ref[i]

        @pl.when(index >= hub_base)
        def _():
            rows = pl.ds(pl.multiple_of((index - hub_base) * TB, TB), TB)
            pltpu.make_async_copy(hub_kv.at[rows], tile_ref.at[i], tile_sem.at[i]).start()

    loads[1].wait()
    scale = 1.0 / head_dim**0.5
    group = max(head_dim, 128)
    per = group // head_dim
    lane = lax.broadcasted_iota(jnp.int32, (TB, group), 1)
    for r in range(local):
        for t in range(tiles):
            i = r * tiles + t
            pltpu.make_async_copy(hub_kv.at[0:TB], tile_ref.at[i], tile_sem.at[i]).wait()
        edges = jnp.concatenate([mask[r, t].astype(jnp.float32) for t in range(tiles)], axis=1)
        for g in range(heads // per):
            cols = slice(g * group, (g + 1) * group)
            keys = tile_ref[r * tiles : (r + 1) * tiles, :, cols].reshape(tiles * TB, group)
            values = tile_ref[
                r * tiles : (r + 1) * tiles, :, width + g * group : width + (g + 1) * group
            ].reshape(tiles * TB, group)
            query = query_ref[r * TB : (r + 1) * TB, cols]
            result = None
            for s in range(per):
                here = (lane >= s * head_dim) & (lane < (s + 1) * head_dim)
                own = query if per == 1 else jnp.where(here, query.astype(jnp.float32), 0.0).astype(jnp.bfloat16)
                score = lax.dot_general(
                    own, keys, (((1,), (1,)), ((), ())), preferred_element_type=jnp.float32
                )
                weight = jnp.exp(score * scale) * edges
                total = jnp.sum(weight, axis=1, keepdims=True)
                summed = jnp.dot(
                    weight.astype(jnp.bfloat16), values, preferred_element_type=jnp.float32
                )
                one = summed / total
                result = one if result is None else jnp.where(here, one, result)
            attn[r * TB : (r + 1) * TB, cols] = result.astype(jnp.bfloat16)
    loads[2].wait()
    mid = tokens_ref[...].astype(jnp.float32) + jnp.dot(
        attn[...], w_out[...], preferred_element_type=jnp.float32
    )
    normed = layer_norm(mid)
    loads[3].wait()
    up = jnp.dot(normed, w_up[...], preferred_element_type=jnp.float32)
    hidden = (0.5 * up * (1.0 + lax.erf(up * (0.5**0.5)))).astype(jnp.bfloat16)
    loads[4].wait()
    out_ref[...] = (
        mid + jnp.dot(hidden, w_down[...], preferred_element_type=jnp.float32)
    ).astype(jnp.bfloat16)


def finish(plan, tokens, query, hub_a, hub_b, mask, w_qkv, w_out, w_up, w_down, stores, heads, head_dim, hub_count):
    node_dev, width = tokens.shape
    local = node_dev // TB
    tiles = mask.shape[1]
    slots = local * tiles
    bf16 = jnp.bfloat16
    return pl.pallas_call(
        functools.partial(final_kernel, heads, head_dim, hub_count, tiles, len(stores)),
        out_shape=jax.ShapeDtypeStruct(tokens.shape, bf16),
        in_specs=[pl.BlockSpec(memory_space=pltpu.SMEM)] + [VMEM] * 4 + [ANY] * (5 + len(stores)),
        out_specs=VMEM,
        scratch_shapes=[
            pltpu.VMEM((slots, TB, 2 * width), bf16),
            pltpu.VMEM((hub_count * TB, 2 * width), bf16),
            pltpu.VMEM((hub_count * TB, width), bf16),
            pltpu.VMEM((local,) + mask.shape[1:], jnp.int32),
            pltpu.VMEM(w_qkv.shape, bf16),
            pltpu.VMEM(w_out.shape, bf16),
            pltpu.VMEM(w_up.shape, bf16),
            pltpu.VMEM(w_down.shape, bf16),
            pltpu.VMEM((node_dev, width), bf16),
            pltpu.SemaphoreType.DMA((slots,)),
            pltpu.SemaphoreType.DMA((5,)),
        ],
        compiler_params=pltpu.CompilerParams(vmem_limit_bytes=40 << 20),
        name="finish",
    )(plan, tokens, query, hub_a, hub_b, mask, w_qkv, w_out, w_up, w_down, *stores)


def body(tokens, w_qkv, w_out, w_up, w_down, tile_cols, tile_mask, hub_blocks):
    node_dev, width = tokens.shape
    nodes = lax.axis_size("nodes")
    heads = lax.axis_size("heads")
    head_dim = width // heads
    per_group, tiles = tile_cols.shape
    hub_count = hub_blocks.shape[0]
    local = node_dev // TB
    here = lax.axis_index("nodes")
    head_here = lax.axis_index("heads")
    go = functools.partial(send, nodes=nodes, heads=heads)

    def core(value):
        return go(value, where=lambda n, h: (n, h ^ 1))

    def pair(value):
        return go(value, where=lambda n, h: (n ^ 1, h))

    def along(value):
        return go(value, where=lambda n, h: (n + 2 - 4 * (n & 1), h))

    strip_at = ((1 - here % 2) * 4 + ((head_here % 4) ^ 2) // 2 * 2) * PIECE
    strip = lax.dynamic_slice_in_dim(tokens.reshape(local, TB, width), strip_at, 2 * PIECE, 1)
    strip = strip.reshape(local * 2 * PIECE, width)
    paired = pair(tokens)
    sides = [go(tokens, where=lambda n, h, o=o: (n, h ^ o)) for o in range(2, heads, 2)]
    across = go(strip, where=lambda n, h: (n ^ 1, h ^ 2))
    token_core = core(tokens)
    paired, *sides, across = lax.optimization_barrier((paired, *sides, across))
    paired_core = core(paired)
    sides_core = [core(v) for v in sides]
    across_core = core(across)

    owner_n = hub_blocks // per_group
    owner_h = hub_blocks % per_group // local
    whole_bits = nodes // 2 * (heads // 4)
    owner_area = owner_n // 2 * (heads // 4) + owner_h // 4
    area = here // 2 * (heads // 4) + head_here // 4
    offset = ((owner_n ^ here) & 1) * 4 + ((owner_h ^ head_here) & 3)
    code = jnp.where(owner_area == area, offset, 8)
    my_piece = here % 2 * 4 + head_here % 4
    pick_plan = jnp.concatenate(
        [
            jnp.stack([code, hub_blocks % local], axis=1).reshape(-1),
            jnp.stack([my_piece, head_here % 2]),
        ]
    ).astype(jnp.int32)
    sources = [tokens, token_core, sides[0], sides_core[0], paired, paired_core, across, across_core]
    piece = pick_pieces(pick_plan, sources, hub_count)

    far = along(paired)
    paired_sides = [pair(v) for v in sides]

    def to_area(n, h, shift):
        at = (n // 2 * (heads // 4) + h // 4) ^ shift
        return at // (heads // 4) * 2 + n % 2, at % (heads // 4) * 4 + h % 4

    step = 1
    apart = owner_area ^ area
    while step < whole_bits:
        reach = [s * step for s in (1, 2, 3) if s * step < whole_bits]
        got = [go(piece, where=lambda n, h, s=s: to_area(n, h, s)) for s in reach]
        digit = jnp.repeat(apart // step % 4, PIECE)[:, None]
        for s, value in zip(reach, got):
            piece = jnp.where(digit == s // step, value, piece)
        step *= 4

    far_sides = [along(v) for v in paired_sides]
    around = [
        piece,
        go(piece, where=lambda n, h: (n, h ^ 2)),
        pair(piece),
        go(piece, where=lambda n, h: (n ^ 1, h ^ 2)),
    ]
    hub_a = jnp.concatenate(around, axis=0)
    hub_b = core(hub_a)

    far_core = core(far)
    paired_sides_core = [core(v) for v in paired_sides]
    far_sides_core = [core(v) for v in far_sides]

    weights = w_qkv
    if head_dim % 128:
        weights = w_qkv.reshape(width, heads, 3, head_dim).swapaxes(1, 2).reshape(width, 3 * width)
    keyval = functools.partial(keyvals, w_qkv=weights, heads=heads, head_dim=head_dim)
    first, query = keyval(tokens, token_core, with_query=True)
    stores = [first]
    for value, other in zip(sides, sides_core):
        stores += keyval(value, other, with_query=False)
    stores += keyval(paired, paired_core, with_query=False)
    for value, other in zip(paired_sides, paired_sides_core):
        stores += keyval(value, other, with_query=False)
    stores += keyval(far, far_core, with_query=False)
    for value, other in zip(far_sides, far_sides_core):
        stores += keyval(value, other, with_query=False)

    mine = lax.dynamic_slice_in_dim(tile_cols, head_here * local, local, 0)
    blocks_all = per_group * nodes
    col_group = mine // per_group
    col_block = mine % per_group
    region = jnp.where(col_group == here, 0, jnp.where(col_group == (here ^ 1), 1, 2))
    index = region * per_group + ((col_block // local) ^ head_here) * local + col_block % local
    hub_slot = jnp.clip(mine - blocks_all, 0, hub_count - 1)
    index = jnp.where(mine >= blocks_all, 3 * per_group + hub_slot, index).reshape(-1)
    offsets = jnp.array([0, 1, 2, 3, 4, 5, 6, 7], jnp.int32)
    plan = jnp.concatenate([index, head_here[None], offsets ^ my_piece]).astype(jnp.int32)
    return finish(
        plan, tokens, query, hub_a, hub_b, tile_mask, weights, w_out, w_up, w_down, stores, heads, head_dim, hub_count
    )


def solution(mesh):
    placed = (
        P(("nodes", "heads"), None),
        P(),
        P(),
        P(),
        P(),
        P("nodes", None),
        P("nodes", None, None, None),
        P(),
    )
    return jax.shard_map(
        body, mesh=mesh, in_specs=placed, out_specs=P(("nodes", "heads"), None), check_vma=False
    )
```

```python
import functools

import jax
import jax.numpy as jnp
from jax import lax
from jax.experimental import pallas as pl
from jax.experimental.pallas import tpu as pltpu
from jax.sharding import PartitionSpec as P

TB = 128
PIECES = 8
PIECE = TB // PIECES
AXES = ("nodes", "heads")
ANY = pl.BlockSpec(memory_space=pl.ANY)
VMEM = pl.BlockSpec(memory_space=pltpu.VMEM)


def send(value, nodes, heads, where):
    pairs = []
    for n in range(nodes):
        for h in range(heads):
            to_n, to_h = where(n, h)
            pairs.append((n * heads + h, to_n % nodes * heads + to_h))
    return lax.ppermute(value, AXES, pairs)


def layer_norm(value_rows):
    mean = jnp.mean(value_rows, axis=-1, keepdims=True)
    centered = value_rows - mean
    spread = jnp.mean(centered * centered, axis=-1, keepdims=True)
    return (centered * lax.rsqrt(spread + 1e-05)).astype(jnp.bfloat16)


def project(normed, w_ref, cols):
    return jnp.dot(normed, w_ref[:, cols], preferred_element_type=jnp.float32).astype(
        jnp.bfloat16
    )


def keyval_into(out_ref, rows, normed, w_ref, heads, head_dim):
    width = heads * head_dim
    if head_dim % 128 == 0:
        for h in range(heads):
            both = project(normed, w_ref, slice((3 * h + 1) * head_dim, (3 * h + 3) * head_dim))
            out_ref[rows, h * head_dim : (h + 1) * head_dim] = both[:, :head_dim]
            out_ref[rows, width + h * head_dim : width + (h + 1) * head_dim] = both[:, head_dim:]
    else:
        out_ref[rows, :] = project(normed, w_ref, slice(width, 3 * width))


def query_into(out_ref, normed, w_ref, heads, head_dim):
    if head_dim % 128 == 0:
        for h in range(heads):
            out_ref[:, h * head_dim : (h + 1) * head_dim] = project(
                normed, w_ref, slice(3 * h * head_dim, (3 * h + 1) * head_dim)
            )
    else:
        out_ref[...] = project(normed, w_ref, slice(0, heads * head_dim))


def keyval_kernel(heads, head_dim, node_dev, first_ref, second_ref, w_ref, out_ref, *query_ref):
    for at, ref in enumerate((first_ref, second_ref)):
        normed = layer_norm(ref[:node_dev, :].astype(jnp.float32))
        keyval_into(out_ref, slice(at * node_dev, (at + 1) * node_dev), normed, w_ref, heads, head_dim)
        if at == 0 and query_ref:
            query_into(query_ref[0], normed, w_ref, heads, head_dim)


def keyvals(first, second, w_qkv, heads, head_dim, node_dev, with_query=False):
    width = first.shape[1]
    out_shape = [jax.ShapeDtypeStruct((2 * node_dev, 2 * width), jnp.bfloat16)]
    if with_query:
        out_shape.append(jax.ShapeDtypeStruct((node_dev, width), jnp.bfloat16))
    return pl.pallas_call(
        functools.partial(keyval_kernel, heads, head_dim, node_dev),
        out_shape=out_shape,
        in_specs=[VMEM] * 3,
        out_specs=[VMEM] * len(out_shape),
        compiler_params=pltpu.CompilerParams(vmem_limit_bytes=8 << 20),
        cost_estimate=pl.CostEstimate(
            flops=64 * node_dev * width * width, bytes_accessed=6 * width * width, transcendentals=0
        ),
        name="keyvals",
    )(first, second, w_qkv)


def place():
    return lax.axis_index("nodes"), lax.axis_index("heads")


def copy_chosen(code, sources, out_ref, out_rows):
    for k, (ref, row) in enumerate(sources):
        @pl.when(code == k)
        def _():
            rows = pl.ds(pl.multiple_of(row, PIECE), PIECE)
            out_ref[out_rows, :] = ref[rows, :]


def pick_kernel(hub_count, per_group, local, heads, hubs_ref, *refs):
    *sources, piece_ref = refs
    here, head_here = place()
    piece = here % 2 * 4 + head_here % 4
    for j in range(hub_count):
        owner_n = hubs_ref[j] // per_group
        owner_h = hubs_ref[j] % per_group // local
        slot = hubs_ref[j] % local
        far = (owner_n // 2 != here // 2) | (owner_h // 4 != head_here // 4)
        offset = (owner_n + here) % 2 * 4 + ((owner_h % 4) ^ (head_here % 4))
        code = jnp.where(far, -1, offset)
        whole = slot * TB + piece * PIECE
        strip = slot * 2 * PIECE + head_here % 2 * PIECE
        rows = slice(j * PIECE, (j + 1) * PIECE)
        copy_chosen(code, [(ref, whole if k < 6 else strip) for k, ref in enumerate(sources)], piece_ref, rows)

        @pl.when(far)
        def _():
            piece_ref[rows, :] = jnp.zeros((PIECE, piece_ref.shape[1]), piece_ref.dtype)


def pick_pieces(hub_blocks, sources, per_group, heads):
    node_dev, width = sources[0].shape
    hub_count = hub_blocks.shape[0]
    return pl.pallas_call(
        functools.partial(pick_kernel, hub_count, per_group, node_dev // TB, heads),
        out_shape=jax.ShapeDtypeStruct((hub_count * PIECE, width), jnp.bfloat16),
        in_specs=[pl.BlockSpec(memory_space=pltpu.SMEM)] + [VMEM] * 8,
        out_specs=VMEM,
        compiler_params=pltpu.CompilerParams(vmem_limit_bytes=4 << 20),
        name="pick_pieces",
    )(hub_blocks, *sources)


def choose_kernel(hub_count, from_where, hubs_ref, *refs):
    *sources, piece_ref = refs
    here, head_here = place()
    for j in range(hub_count):
        code = from_where(hubs_ref[j], here, head_here)
        rows = slice(j * PIECE, (j + 1) * PIECE)
        copy_chosen(code, [(ref, j * PIECE) for ref in sources], piece_ref, rows)


def choose_pieces(hub_blocks, sources, from_where):
    return pl.pallas_call(
        functools.partial(choose_kernel, hub_blocks.shape[0], from_where),
        out_shape=jax.ShapeDtypeStruct(sources[0].shape, jnp.bfloat16),
        in_specs=[pl.BlockSpec(memory_space=pltpu.SMEM)] + [VMEM] * len(sources),
        out_specs=VMEM,
        compiler_params=pltpu.CompilerParams(vmem_limit_bytes=4 << 20),
        name="choose_pieces",
    )(hub_blocks, *sources)


def final_kernel(
    heads, head_dim, hub_count, per_group, nodes, count,
    cols_ref, tokens_ref, query_ref, mask_ref, w_qkv_ref, w_out_ref, w_up_ref, w_down_ref, *refs
):
    around, refs = refs[:PIECES], refs[PIECES:]
    stores, out_ref = refs[:count], refs[count]
    tile_ref, hub_kv, hub_rows, mask, w_qkv, w_out, w_up, w_down, attn, tile_sem, sem = refs[count + 1 :]
    node_dev, width = tokens_ref.shape
    local = node_dev // TB
    tiles = mask_ref.shape[1]
    slots = local * tiles
    in_store = stores[0].shape[0] // TB
    here, head_here = place()
    hub_base = count * in_store
    indices = []
    for i in range(slots):
        col = cols_ref[head_here * local + i // tiles, i % tiles]
        group, block = col // per_group, col % per_group
        region = jnp.where(group == here, 0, jnp.where(group // 2 == here // 2, 1, 2))
        index = region * per_group + ((block // local) ^ head_here) * local + block % local
        indices.append(jnp.where(col >= nodes * per_group, hub_base + col - nodes * per_group, index))
    loads = [
        pltpu.make_async_copy(w_qkv_ref, w_qkv, sem.at[0]),
        pltpu.make_async_copy(
            mask_ref.at[pl.ds(head_here * local, local)], mask, sem.at[1]
        ),
        pltpu.make_async_copy(w_out_ref, w_out, sem.at[2]),
        pltpu.make_async_copy(w_up_ref, w_up, sem.at[3]),
        pltpu.make_async_copy(w_down_ref, w_down, sem.at[4]),
    ]
    loads[0].start()
    for i in range(slots):
        index = indices[i]
        for a, store in enumerate(stores):
            @pl.when(index // in_store == a)
            def _():
                rows = pl.ds(pl.multiple_of(index % in_store * TB, TB), TB)
                pltpu.make_async_copy(store.at[rows], tile_ref.at[i], tile_sem.at[i]).start()

    for load in loads[1:]:
        load.start()
    mine = here % 2 * 4 + head_here % 4
    for k, ref in enumerate(around):
        for j in range(hub_count):
            row = ref.shape[0] - (hub_count - j) * PIECE
            rows = pl.ds(pl.multiple_of(j * TB + (mine ^ k) * PIECE, PIECE), PIECE)
            hub_rows[rows, :] = ref[row : row + PIECE, :]
    hub_normed = layer_norm(hub_rows[...].astype(jnp.float32))
    loads[0].wait()
    keyval_into(hub_kv, slice(None), hub_normed, w_qkv, heads, head_dim)
    for i in range(slots):
        index = indices[i]

        @pl.when(index >= hub_base)
        def _():
            rows = pl.ds(pl.multiple_of((index - hub_base) * TB, TB), TB)
            pltpu.make_async_copy(hub_kv.at[rows], tile_ref.at[i], tile_sem.at[i]).start()

    loads[1].wait()
    scale = 1.0 / head_dim**0.5
    group = max(head_dim, 128)
    per = group // head_dim
    lane = lax.broadcasted_iota(jnp.int32, (TB, group), 1)
    for r in range(local):
        for t in range(tiles):
            i = r * tiles + t
            pltpu.make_async_copy(hub_kv.at[0:TB], tile_ref.at[i], tile_sem.at[i]).wait()
        edges = jnp.concatenate([mask[r, t].astype(jnp.float32) for t in range(tiles)], axis=1)
        for g in range(heads // per):
            cols = slice(g * group, (g + 1) * group)
            keys = tile_ref[r * tiles : (r + 1) * tiles, :, cols].reshape(tiles * TB, group)
            values = tile_ref[
                r * tiles : (r + 1) * tiles, :, width + g * group : width + (g + 1) * group
            ].reshape(tiles * TB, group)
            query = query_ref[r * TB : (r + 1) * TB, cols]
            result = None
            for s in range(per):
                here = (lane >= s * head_dim) & (lane < (s + 1) * head_dim)
                own = query if per == 1 else jnp.where(here, query.astype(jnp.float32), 0.0).astype(jnp.bfloat16)
                score = lax.dot_general(
                    own, keys, (((1,), (1,)), ((), ())), preferred_element_type=jnp.float32
                )
                weight = jnp.exp(score * scale) * edges
                total = jnp.sum(weight, axis=1, keepdims=True)
                summed = jnp.dot(
                    weight.astype(jnp.bfloat16), values, preferred_element_type=jnp.float32
                )
                one = summed / total
                result = one if result is None else jnp.where(here, one, result)
            attn[r * TB : (r + 1) * TB, cols] = result.astype(jnp.bfloat16)
    loads[2].wait()
    mid = tokens_ref[...].astype(jnp.float32) + jnp.dot(
        attn[...], w_out[...], preferred_element_type=jnp.float32
    )
    normed = layer_norm(mid)
    loads[3].wait()
    up = jnp.dot(normed, w_up[...], preferred_element_type=jnp.float32)
    hidden = (0.5 * up * (1.0 + lax.erf(up * (0.5**0.5)))).astype(jnp.bfloat16)
    loads[4].wait()
    out_ref[...] = (
        mid + jnp.dot(hidden, w_down[...], preferred_element_type=jnp.float32)
    ).astype(jnp.bfloat16)


def finish(cols, tokens, query, mask, w_qkv, w_out, w_up, w_down, around, stores, heads, head_dim, hub_count, nodes):
    node_dev, width = tokens.shape
    local = node_dev // TB
    tiles = mask.shape[1]
    slots = local * tiles
    bf16 = jnp.bfloat16
    return pl.pallas_call(
        functools.partial(final_kernel, heads, head_dim, hub_count, cols.shape[0], nodes, len(stores)),
        out_shape=jax.ShapeDtypeStruct(tokens.shape, bf16),
        in_specs=[pl.BlockSpec(memory_space=pltpu.SMEM)] + [VMEM] * 2 + [ANY] * 5 + [VMEM] * PIECES + [ANY] * len(stores),
        out_specs=VMEM,
        scratch_shapes=[
            pltpu.VMEM((slots, TB, 2 * width), bf16),
            pltpu.VMEM((hub_count * TB, 2 * width), bf16),
            pltpu.VMEM((hub_count * TB, width), bf16),
            pltpu.VMEM((local,) + mask.shape[1:], jnp.int32),
            pltpu.VMEM(w_qkv.shape, bf16),
            pltpu.VMEM(w_out.shape, bf16),
            pltpu.VMEM(w_up.shape, bf16),
            pltpu.VMEM(w_down.shape, bf16),
            pltpu.VMEM((node_dev, width), bf16),
            pltpu.SemaphoreType.DMA((slots,)),
            pltpu.SemaphoreType.DMA((5,)),
        ],
        compiler_params=pltpu.CompilerParams(vmem_limit_bytes=28 << 20),
        name="finish",
    )(cols, tokens, query, mask, w_qkv, w_out, w_up, w_down, *around, *stores)


def body(tokens, w_qkv, w_out, w_up, w_down, tile_cols, tile_mask, hub_blocks):
    node_dev, width = tokens.shape
    nodes = lax.axis_size("nodes")
    heads = lax.axis_size("heads")
    head_dim = width // heads
    per_group = tile_cols.shape[0]
    hub_count = hub_blocks.shape[0]
    local = node_dev // TB
    in_row = heads // 4
    areas = nodes // 2 * in_row
    go = functools.partial(send, nodes=nodes, heads=heads)

    def core(value):
        return go(value, where=lambda n, h: (n, h ^ 1))

    def pair(value):
        return go(value, where=lambda n, h: (n ^ 1, h))

    def across(value):
        return go(value, where=lambda n, h: (n ^ 1, h ^ 2))

    def side(value, offset=2):
        return go(value, where=lambda n, h: (n, h ^ offset))

    def along(value, by=1):
        return go(value, where=lambda n, h: (n + (2 - 4 * (n & 1)) * by, h))

    weights = w_qkv
    if head_dim % 128:
        weights = w_qkv.reshape(width, heads, 3, head_dim).swapaxes(1, 2).reshape(width, 3 * width)
    keyval = functools.partial(keyvals, w_qkv=weights, heads=heads, head_dim=head_dim, node_dev=node_dev)

    other = range(2, heads, 2)
    sides = [side(tokens, o) for o in other]
    paired = pair(tokens)
    here, head_here = place()
    strip_at = ((1 - here % 2) * 4 + ((head_here % 4) ^ 2) // 2 * 2) * PIECE
    strip = lax.dynamic_slice_in_dim(tokens.reshape(local, TB, width), strip_at, 2 * PIECE, 1)
    strip = across(strip.reshape(local * 2 * PIECE, width))
    token_core = core(tokens)
    first, query = keyval(tokens, token_core, with_query=True)
    paired, strip, first, query, *sides = lax.optimization_barrier((paired, strip, first, query, *sides))

    paired_core, strip_core = core(paired), core(strip)
    sides_core = [core(v) for v in sides]
    sources = [tokens, token_core, sides[0], sides_core[0], paired, paired_core, strip, strip_core]
    far = along(paired)
    piece = pick_pieces(hub_blocks, sources, per_group, heads)

    piece, *onward = lax.optimization_barrier((piece, *sides))
    paired_sides = [pair(v) for v in onward]
    stores = [first]
    stores += [keyval(v, c)[0] for v, c in zip(sides, sides_core)]
    stores += list(keyval(paired, paired_core))

    def owner_area(block):
        return block // per_group // 2 * in_row + block % per_group // local // 4

    def area_of(here, head_here):
        return here // 2 * in_row + head_here // 4

    if areas == 4 and in_row == 1:
        got = [piece, along(piece), along(piece, 2), along(piece, -1)]
        got, stores, far = lax.optimization_barrier((got, stores, far))

        def from_where(block, here, head_here):
            ahead = area_of(here, head_here) + 4 - owner_area(block)
            return jnp.where(here % 2 == 0, ahead, 8 - ahead) % 4

        piece = choose_pieces(hub_blocks, got, from_where)
    else:

        def to_area(n, h, shift):
            at = (n // 2 * in_row + h // 4) ^ shift
            return at // in_row * 2 + n % 2, at % in_row * 4 + h % 4

        step = 1
        while step < areas:
            reach = [s * step for s in (1, 2, 3) if s * step < areas]
            got = [go(piece, where=lambda n, h, s=s: to_area(n, h, s)) for s in reach]

            def from_where(block, here, head_here, step=step):
                return (owner_area(block) ^ area_of(here, head_here)) // step % 4

            piece = choose_pieces(hub_blocks, [piece, *got], from_where)
            step *= 4

    far_sides = [side(far, o) for o in other]
    around = [piece, side(piece), pair(piece), across(piece)]
    far_core = core(far)
    paired_sides_core = [core(v) for v in paired_sides]
    stores += [keyval(v, c)[0] for v, c in zip(paired_sides, paired_sides_core)]
    stores += list(keyval(far, far_core))
    around, stores, far_sides = lax.optimization_barrier((around, stores, far_sides))
    far_sides_core = [core(v) for v in far_sides]
    stores += [keyval(v, c)[0] for v, c in zip(far_sides, far_sides_core)]

    around = [v for value in around for v in (value, core(value))]
    return finish(
        tile_cols, tokens, query, tile_mask, weights, w_out, w_up, w_down, around, stores, heads, head_dim, hub_count, nodes
    )


def solution(mesh):
    placed = (
        P(("nodes", "heads"), None),
        P(),
        P(),
        P(),
        P(),
        P("nodes", None),
        P("nodes", None, None, None),
        P(),
    )
    return jax.shard_map(
        body, mesh=mesh, in_specs=placed, out_specs=P(("nodes", "heads"), None), check_vma=False
    )
```

```python
import functools

import jax
import jax.numpy as jnp
from jax import lax
from jax.experimental import pallas as pl
from jax.experimental.pallas import tpu as pltpu
from jax.sharding import PartitionSpec as P

TB = 128
PIECES = 8
PIECE = TB // PIECES
AXES = ("nodes", "heads")
ANY = pl.BlockSpec(memory_space=pl.ANY)
VMEM = pl.BlockSpec(memory_space=pltpu.VMEM)


def send(value, nodes, heads, where):
    pairs = []
    for n in range(nodes):
        for h in range(heads):
            to_n, to_h = where(n, h)
            pairs.append((n * heads + h, to_n % nodes * heads + to_h))
    return lax.ppermute(value, AXES, pairs)


def layer_norm(value_rows):
    mean = jnp.mean(value_rows, axis=-1, keepdims=True)
    centered = value_rows - mean
    spread = jnp.mean(centered * centered, axis=-1, keepdims=True)
    return (centered * lax.rsqrt(spread + 1e-05)).astype(jnp.bfloat16)


def project(normed, w_ref, cols):
    return jnp.dot(normed, w_ref[:, cols], preferred_element_type=jnp.float32).astype(
        jnp.bfloat16
    )


def keyval_into(out_ref, rows, normed, w_ref, heads, head_dim):
    width = heads * head_dim
    if head_dim % 128 == 0:
        for h in range(heads):
            both = project(normed, w_ref, slice((3 * h + 1) * head_dim, (3 * h + 3) * head_dim))
            out_ref[rows, h * head_dim : (h + 1) * head_dim] = both[:, :head_dim]
            out_ref[rows, width + h * head_dim : width + (h + 1) * head_dim] = both[:, head_dim:]
    else:
        out_ref[rows, :] = project(normed, w_ref, slice(width, 3 * width))


def query_into(out_ref, normed, w_ref, heads, head_dim):
    if head_dim % 128 == 0:
        for h in range(heads):
            out_ref[:, h * head_dim : (h + 1) * head_dim] = project(
                normed, w_ref, slice(3 * h * head_dim, (3 * h + 1) * head_dim)
            )
    else:
        out_ref[...] = project(normed, w_ref, slice(0, heads * head_dim))


def keyval_kernel(heads, head_dim, at, first_ref, second_ref, w_ref, *refs):
    node_dev = first_ref.shape[0]
    pool_ref = refs[-1] if at else refs[-3]
    for k, ref in enumerate((first_ref, second_ref)):
        normed = layer_norm(ref[...].astype(jnp.float32))
        rows = slice((at + k) * node_dev, (at + k + 1) * node_dev)
        keyval_into(pool_ref, rows, normed, w_ref, heads, head_dim)
        if not at and not k:
            query_into(refs[-2], normed, w_ref, heads, head_dim)
            refs[-1][...] = ref[...]


def keyvals(pool, at, first, second, w_qkv, heads, head_dim, blocks, after=()):
    node_dev, width = first.shape
    out_shape = [jax.ShapeDtypeStruct((blocks * TB, 2 * width), jnp.bfloat16)]
    if not at:
        out_shape += [jax.ShapeDtypeStruct((node_dev, width), jnp.bfloat16)] * 2
    operands = [first, second, w_qkv, *after] + ([pool] if at else [])
    result = pl.pallas_call(
        functools.partial(keyval_kernel, heads, head_dim, at),
        out_shape=out_shape,
        in_specs=[VMEM] * 3 + [ANY] * len(after) + [VMEM] * bool(at),
        out_specs=[VMEM] * len(out_shape),
        input_output_aliases={len(operands) - 1: 0} if at else {},
        compiler_params=pltpu.CompilerParams(vmem_limit_bytes=8 << 20),
        cost_estimate=pl.CostEstimate(
            flops=64 * node_dev * width * width, bytes_accessed=6 * width * width, transcendentals=0
        ),
        name="keyvals",
    )(*operands)
    return result if not at else result[0]


def place():
    return lax.axis_index("nodes"), lax.axis_index("heads")


def copy_chosen(code, sources, out_ref, out_rows):
    for k, (ref, row) in enumerate(sources):
        @pl.when(code == k)
        def _():
            rows = pl.ds(pl.multiple_of(row, PIECE), PIECE)
            out_ref[out_rows, :] = ref[rows, :]


def pick_kernel(hub_count, per_group, local, heads, hubs_ref, *refs):
    *sources, piece_ref = refs
    here, head_here = place()
    piece = here % 2 * 4 + head_here % 4
    for j in range(hub_count):
        owner_n = hubs_ref[j] // per_group
        owner_h = hubs_ref[j] % per_group // local
        slot = hubs_ref[j] % local
        far = (owner_n // 2 != here // 2) | (owner_h // 4 != head_here // 4)
        offset = (owner_n + here) % 2 * 4 + ((owner_h % 4) ^ (head_here % 4))
        code = jnp.where(far, -1, offset)
        whole = slot * TB + piece * PIECE
        strip = slot * 2 * PIECE + head_here % 2 * PIECE
        rows = slice(j * PIECE, (j + 1) * PIECE)
        copy_chosen(code, [(ref, whole if k < 6 else strip) for k, ref in enumerate(sources)], piece_ref, rows)

        @pl.when(far)
        def _():
            piece_ref[rows, :] = jnp.zeros((PIECE, piece_ref.shape[1]), piece_ref.dtype)


def pick_pieces(hub_blocks, sources, per_group, heads):
    node_dev, width = sources[0].shape
    hub_count = hub_blocks.shape[0]
    return pl.pallas_call(
        functools.partial(pick_kernel, hub_count, per_group, node_dev // TB, heads),
        out_shape=jax.ShapeDtypeStruct((hub_count * PIECE, width), jnp.bfloat16),
        in_specs=[pl.BlockSpec(memory_space=pltpu.SMEM)] + [VMEM] * 8,
        out_specs=VMEM,
        compiler_params=pltpu.CompilerParams(vmem_limit_bytes=4 << 20),
        name="pick_pieces",
    )(hub_blocks, *sources)


def choose_kernel(hub_count, from_where, hubs_ref, *refs):
    *sources, piece_ref = refs
    here, head_here = place()
    for j in range(hub_count):
        code = from_where(hubs_ref[j], here, head_here)
        rows = slice(j * PIECE, (j + 1) * PIECE)
        copy_chosen(code, [(ref, j * PIECE) for ref in sources], piece_ref, rows)


def choose_pieces(hub_blocks, sources, from_where):
    return pl.pallas_call(
        functools.partial(choose_kernel, hub_blocks.shape[0], from_where),
        out_shape=jax.ShapeDtypeStruct(sources[0].shape, jnp.bfloat16),
        in_specs=[pl.BlockSpec(memory_space=pltpu.SMEM)] + [VMEM] * len(sources),
        out_specs=VMEM,
        compiler_params=pltpu.CompilerParams(vmem_limit_bytes=4 << 20),
        name="choose_pieces",
    )(hub_blocks, *sources)


def finish_kernel(
    heads, head_dim, hub_count, hub_base, cols_ref,
    tokens_ref, query_ref, mask_ref, w_qkv_ref, w_out_ref, w_up_ref, w_down_ref, *refs
):
    around, (_, out_ref, pool_ref, hub_rows, mask, attn, sem) = refs[:PIECES], refs[PIECES:]
    node_dev, width = tokens_ref.shape
    local = node_dev // TB
    per_group, tiles = cols_ref.shape
    here, head_here = place()
    load = pltpu.make_async_copy(mask_ref.at[pl.ds(head_here * local, local)], mask, sem)
    load.start()
    mine = here % 2 * 4 + head_here % 4
    for k, ref in enumerate(around):
        for j in range(hub_count):
            row = ref.shape[0] - (hub_count - j) * PIECE
            rows = pl.ds(pl.multiple_of(j * TB + (mine ^ k) * PIECE, PIECE), PIECE)
            hub_rows[rows, :] = ref[row : row + PIECE, :]
    hub_normed = layer_norm(hub_rows[...].astype(jnp.float32))
    hub_place = pool_ref.shape[0] // TB - hub_count
    keyval_into(pool_ref, slice(hub_place * TB, None), hub_normed, w_qkv_ref, heads, head_dim)
    load.wait()
    group = max(head_dim, 128)
    for r in range(local):
        rows = slice(r * TB, (r + 1) * TB)
        places = []
        for t in range(tiles):
            col = cols_ref[head_here * local + r, t]
            near, block = col // per_group, col % per_group
            region = jnp.where(near == here, 0, jnp.where(near // 2 == here // 2, 1, 2))
            index = region * per_group + ((block // local) ^ head_here) * local + block % local
            index = jnp.where(col < hub_base, index, hub_place + col - hub_base)
            places.append(pl.ds(pl.multiple_of(index * TB, TB), TB))
        edges = jnp.concatenate([mask[r, t].astype(jnp.float32) for t in range(tiles)], axis=1)
        for g in range(width // group):
            cols = slice(g * group, (g + 1) * group)
            beyond = slice(width + g * group, width + (g + 1) * group)
            keys = jnp.concatenate([pool_ref[at, cols] for at in places], axis=0)
            values = jnp.concatenate([pool_ref[at, beyond] for at in places], axis=0)
            attn[rows, cols] = attention(query_ref[rows, cols], keys, values, edges, head_dim)
    mid = tokens_ref[...].astype(jnp.float32) + jnp.dot(
        attn[...], w_out_ref[...], preferred_element_type=jnp.float32
    )
    normed = layer_norm(mid)
    up = jnp.dot(normed, w_up_ref[...], preferred_element_type=jnp.float32)
    hidden = (0.5 * up * (1.0 + lax.erf(up * (0.5**0.5)))).astype(jnp.bfloat16)
    out_ref[...] = (
        mid + jnp.dot(hidden, w_down_ref[...], preferred_element_type=jnp.float32)
    ).astype(jnp.bfloat16)


def attention(query, keys, values, edges, head_dim):
    per = query.shape[1] // head_dim
    scale = 1.0 / head_dim**0.5
    lane = lax.broadcasted_iota(jnp.int32, query.shape, 1)
    result = None
    for s in range(per):
        here = (lane >= s * head_dim) & (lane < (s + 1) * head_dim)
        own = query if per == 1 else jnp.where(here, query.astype(jnp.float32), 0.0).astype(jnp.bfloat16)
        score = lax.dot_general(own, keys, (((1,), (1,)), ((), ())), preferred_element_type=jnp.float32)
        weight = jnp.exp(score * scale) * edges
        total = jnp.sum(weight, axis=1, keepdims=True)
        summed = jnp.dot(weight.astype(jnp.bfloat16), values, preferred_element_type=jnp.float32)
        one = summed / total
        result = one if result is None else jnp.where(here, one, result)
    return result.astype(jnp.bfloat16)


def finish(cols, tokens, query, mask, w_qkv, w_out, w_up, w_down, around, pool, heads, head_dim, hub_count, hub_base):
    node_dev, width = tokens.shape
    bf16 = jnp.bfloat16
    return pl.pallas_call(
        functools.partial(finish_kernel, heads, head_dim, hub_count, hub_base),
        out_shape=[jax.ShapeDtypeStruct(tokens.shape, bf16), jax.ShapeDtypeStruct(pool.shape, bf16)],
        in_specs=[pl.BlockSpec(memory_space=pltpu.SMEM)]
        + [VMEM] * 2
        + [pl.BlockSpec(memory_space=pltpu.HBM)]
        + [VMEM] * (5 + PIECES),
        out_specs=[VMEM, VMEM],
        input_output_aliases={8 + PIECES: 1},
        scratch_shapes=[
            pltpu.VMEM((hub_count * TB, width), bf16),
            pltpu.VMEM((node_dev // TB,) + mask.shape[1:], jnp.int32),
            pltpu.VMEM((node_dev, width), bf16),
            pltpu.SemaphoreType.DMA,
        ],
        compiler_params=pltpu.CompilerParams(vmem_limit_bytes=20 << 20),
        name="finish",
    )(cols, tokens, query, mask, w_qkv, w_out, w_up, w_down, *around, pool)[0]


def body(tokens, w_qkv, w_out, w_up, w_down, tile_cols, tile_mask, hub_blocks):
    node_dev, width = tokens.shape
    nodes = lax.axis_size("nodes")
    heads = lax.axis_size("heads")
    head_dim = width // heads
    per_group = tile_cols.shape[0]
    hub_count = hub_blocks.shape[0]
    local = node_dev // TB
    in_row = heads // 4
    areas = nodes // 2 * in_row
    go = functools.partial(send, nodes=nodes, heads=heads)

    def core(value):
        return go(value, where=lambda n, h: (n, h ^ 1))

    def pair(value):
        return go(value, where=lambda n, h: (n ^ 1, h))

    def across(value):
        return go(value, where=lambda n, h: (n ^ 1, h ^ 2))

    def side(value, offset=2):
        return go(value, where=lambda n, h: (n, h ^ offset))

    def along(value, by=1):
        return go(value, where=lambda n, h: (n + (2 - 4 * (n & 1)) * by, h))

    weights = w_qkv
    if head_dim % 128:
        weights = w_qkv.reshape(width, heads, 3, head_dim).swapaxes(1, 2).reshape(width, 3 * width)
    keyval = functools.partial(
        keyvals, w_qkv=weights, heads=heads, head_dim=head_dim, blocks=3 * per_group + hub_count
    )

    other = range(2, heads, 2)
    sides = [side(tokens, o) for o in other]
    paired = pair(tokens)
    here, head_here = place()
    strip_at = ((1 - here % 2) * 4 + ((head_here % 4) ^ 2) // 2 * 2) * PIECE
    strip = lax.dynamic_slice_in_dim(tokens.reshape(local, TB, width), strip_at, 2 * PIECE, 1)
    strip = across(strip.reshape(local * 2 * PIECE, width))
    token_core = core(tokens)
    pool, query, again = keyval(None, 0, tokens, token_core)
    far = go(again, where=lambda n, h: (n - 1 + 2 * (n & 1), h))
    paired, strip, pool, query, *sides = lax.optimization_barrier((paired, strip, pool, query, *sides))

    paired_core, strip_core = core(paired), core(strip)
    sides_core = [core(v) for v in sides]
    paired_sides = [pair(v) for v in sides]
    sources = [tokens, token_core, sides[0], sides_core[0], paired, paired_core, strip, strip_core]
    piece = pick_pieces(hub_blocks, sources, per_group, heads)

    for k, (value, other_value) in enumerate(zip(sides, sides_core)):
        pool = keyval(pool, 2 + 2 * k, value, other_value, after=(piece,))
    far, pool = lax.optimization_barrier((far, pool))
    far_sides = [side(far, o) for o in other]
    far_core = core(far)
    pool = keyval(pool, heads, paired, paired_core)

    def owner_area(block):
        return block // per_group // 2 * in_row + block % per_group // local // 4

    def area_of(here, head_here):
        return here // 2 * in_row + head_here // 4

    if areas == 4 and in_row == 1:
        got = [piece, along(piece), along(piece, 2), along(piece, -1)]
        got, pool, paired_sides = lax.optimization_barrier((got, pool, paired_sides))

        def from_where(block, here, head_here):
            ahead = area_of(here, head_here) + 4 - owner_area(block)
            return jnp.where(here % 2 == 0, ahead, 8 - ahead) % 4

        piece = choose_pieces(hub_blocks, got, from_where)
    else:

        def to_area(n, h, shift):
            at = (n // 2 * in_row + h // 4) ^ shift
            return at // in_row * 2 + n % 2, at % in_row * 4 + h % 4

        step = 1
        while step < areas:
            reach = [s * step for s in (1, 2, 3) if s * step < areas]
            got = [go(piece, where=lambda n, h, s=s: to_area(n, h, s)) for s in reach]

            def from_where(block, here, head_here, step=step):
                return (owner_area(block) ^ area_of(here, head_here)) // step % 4

            piece = choose_pieces(hub_blocks, [piece, *got], from_where)
            step *= 4

    around = [piece, side(piece), pair(piece), across(piece)]
    paired_sides_core = [core(v) for v in paired_sides]
    far_sides_core = [core(v) for v in far_sides]
    for k, (value, other_value) in enumerate(zip(paired_sides, paired_sides_core)):
        pool = keyval(pool, heads + 2 + 2 * k, value, other_value)
    for k, (value, other_value) in enumerate(zip([far, *far_sides], [far_core, *far_sides_core])):
        pool = keyval(pool, 2 * heads + 2 * k, value, other_value)
    around, pool = lax.optimization_barrier((around, pool))

    around = [v for value in around for v in (value, core(value))]
    return finish(
        tile_cols, tokens, query, tile_mask, weights, w_out, w_up, w_down, around, pool, heads, head_dim, hub_count, per_group * nodes
    )


def solution(mesh):
    placed = (
        P(("nodes", "heads"), None),
        P(),
        P(),
        P(),
        P(),
        P("nodes", None),
        P("nodes", None, None, None),
        P(),
    )
    return jax.shard_map(
        body, mesh=mesh, in_specs=placed, out_specs=P(("nodes", "heads"), None), check_vma=False
    )
```

```python
import functools

import jax
import jax.numpy as jnp
from jax import lax
from jax.experimental import pallas as pl
from jax.experimental.pallas import tpu as pltpu
from jax.sharding import PartitionSpec as P

TB = 128
PIECES = 8
PIECE = TB // PIECES
AXES = ("nodes", "heads")
ANY = pl.BlockSpec(memory_space=pl.ANY)
VMEM = pl.BlockSpec(memory_space=pltpu.VMEM)


def send(value, nodes, heads, where):
    pairs = []
    for n in range(nodes):
        for h in range(heads):
            to_n, to_h = where(n, h)
            pairs.append((n * heads + h, to_n % nodes * heads + to_h))
    return lax.ppermute(value, AXES, pairs)


def layer_norm(value_rows):
    mean = jnp.mean(value_rows, axis=-1, keepdims=True)
    centered = value_rows - mean
    spread = jnp.mean(centered * centered, axis=-1, keepdims=True)
    return (centered * lax.rsqrt(spread + 1e-05)).astype(jnp.bfloat16)


def project(normed, w_ref, cols):
    return jnp.dot(normed, w_ref[:, cols], preferred_element_type=jnp.float32).astype(
        jnp.bfloat16
    )


def keyval_into(out_ref, rows, normed, w_ref, heads, head_dim):
    width = heads * head_dim
    if head_dim % 128 == 0:
        for h in range(heads):
            both = project(normed, w_ref, slice((3 * h + 1) * head_dim, (3 * h + 3) * head_dim))
            out_ref[rows, h * head_dim : (h + 1) * head_dim] = both[:, :head_dim]
            out_ref[rows, width + h * head_dim : width + (h + 1) * head_dim] = both[:, head_dim:]
    else:
        out_ref[rows, :] = project(normed, w_ref, slice(width, 3 * width))


def query_into(out_ref, normed, w_ref, heads, head_dim):
    if head_dim % 128 == 0:
        for h in range(heads):
            out_ref[:, h * head_dim : (h + 1) * head_dim] = project(
                normed, w_ref, slice(3 * h * head_dim, (3 * h + 1) * head_dim)
            )
    else:
        out_ref[...] = project(normed, w_ref, slice(0, heads * head_dim))


def keyval_kernel(heads, head_dim, at, whence, first_ref, second_ref, w_ref, *refs):
    node_dev = first_ref.shape[0]
    pool_ref = refs[-1] if at else refs[-4]
    if not at:
        hubs_ref, codes_ref = refs[0], refs[-1]
        here, head_here = place()
        for j in range(hubs_ref.shape[0]):
            for i, code in enumerate(whence):
                number = code(hubs_ref[j], here, head_here).astype(jnp.float32)
                codes_ref[i, j * PIECE : (j + 1) * PIECE, :] = jnp.full((PIECE, 128), number)
    for k, ref in enumerate((first_ref, second_ref)):
        normed = layer_norm(ref[...].astype(jnp.float32))
        rows = slice((at + k) * node_dev, (at + k + 1) * node_dev)
        keyval_into(pool_ref, rows, normed, w_ref, heads, head_dim)
        if not at and not k:
            query_into(refs[-3], normed, w_ref, heads, head_dim)
            refs[-2][...] = ref[...]


def keyvals(pool, at, first, second, w_qkv, heads, head_dim, blocks, after=(), hub_blocks=None, whence=()):
    node_dev, width = first.shape
    out_shape = [jax.ShapeDtypeStruct((blocks * TB, 2 * width), jnp.bfloat16)]
    if not at:
        out_shape += [jax.ShapeDtypeStruct((node_dev, width), jnp.bfloat16)] * 2
        shape = (len(whence), hub_blocks.shape[0] * PIECE, 128)
        out_shape.append(jax.ShapeDtypeStruct(shape, jnp.float32))
    operands = [first, second, w_qkv, *after] + ([pool] if at else [hub_blocks])
    result = pl.pallas_call(
        functools.partial(keyval_kernel, heads, head_dim, at, whence),
        out_shape=out_shape,
        in_specs=[VMEM] * 3 + [ANY] * len(after) + [VMEM if at else pl.BlockSpec(memory_space=pltpu.SMEM)],
        out_specs=[VMEM] * len(out_shape),
        input_output_aliases={len(operands) - 1: 0} if at else {},
        compiler_params=pltpu.CompilerParams(vmem_limit_bytes=8 << 20),
        cost_estimate=pl.CostEstimate(
            flops=64 * node_dev * width * width, bytes_accessed=6 * width * width, transcendentals=0
        ),
        name="keyvals",
    )(*operands)
    return result if not at else result[0]


def later(value, *first):
    return lax.optimization_barrier((value, *first))[0]


def place():
    return lax.axis_index("nodes"), lax.axis_index("heads")


def chosen(code_ref, at, rows, candidates):
    width = candidates[0].shape[1]
    code = jnp.concatenate([code_ref[at, rows, :]] * (width // 128), axis=1)
    result = candidates[0].astype(jnp.float32)
    for k, value in enumerate(candidates[1:], 1):
        result = jnp.where(code == k, value.astype(jnp.float32), result)
    return result.astype(jnp.bfloat16)


def pick_kernel(hub_count, local, code_ref, *refs):
    *sources, piece_ref = refs
    here, head_here = place()
    piece = here % 2 * 4 + head_here % 4
    candidates = []
    for k, ref in enumerate(sources):
        for slot in range(local):
            row = slot * TB + piece * PIECE if k < 6 else (slot * 2 + head_here % 2) * PIECE
            candidates.append(ref[pl.ds(pl.multiple_of(row, PIECE), PIECE), :])
    for j in range(hub_count):
        rows = slice(j * PIECE, (j + 1) * PIECE)
        piece_ref[rows, :] = chosen(code_ref, 0, rows, candidates)


def pick_pieces(codes, sources):
    node_dev, width = sources[0].shape
    rows = codes.shape[1]
    return pl.pallas_call(
        functools.partial(pick_kernel, rows // PIECE, node_dev // TB),
        out_shape=jax.ShapeDtypeStruct((rows, width), jnp.bfloat16),
        in_specs=[VMEM] * (1 + len(sources)),
        out_specs=VMEM,
        compiler_params=pltpu.CompilerParams(vmem_limit_bytes=4 << 20),
        name="pick_pieces",
    )(codes, *sources)


def choose_kernel(at, code_ref, *refs):
    *sources, piece_ref = refs
    piece_ref[...] = chosen(code_ref, at, slice(None), [ref[...] for ref in sources])


def choose_pieces(codes, at, sources):
    return pl.pallas_call(
        functools.partial(choose_kernel, at),
        out_shape=jax.ShapeDtypeStruct(sources[0].shape, jnp.bfloat16),
        in_specs=[VMEM] * (1 + len(sources)),
        out_specs=VMEM,
        compiler_params=pltpu.CompilerParams(vmem_limit_bytes=4 << 20),
        name="choose_pieces",
    )(codes, *sources)


def finish_kernel(
    heads, head_dim, hub_count, hub_base, cols_ref,
    tokens_ref, query_ref, mask_ref, w_qkv_ref, w_out_ref, w_up_ref, w_down_ref, *refs
):
    around, (_, out_ref, pool_ref, hub_rows, mask, attn, sem) = refs[:2], refs[2:]
    node_dev, width = tokens_ref.shape
    local = node_dev // TB
    per_group, tiles = cols_ref.shape
    here, head_here = place()
    load = pltpu.make_async_copy(mask_ref.at[pl.ds(head_here * local, local)], mask, sem)
    load.start()
    mine = here % 2 * 4 + head_here % 4
    for k in range(PIECES):
        for j in range(hub_count):
            row = (k // 2 * hub_count + j) * PIECE
            rows = pl.ds(pl.multiple_of(j * TB + (mine ^ k) * PIECE, PIECE), PIECE)
            hub_rows[rows, :] = around[k % 2][row : row + PIECE, :]
    hub_normed = layer_norm(hub_rows[...].astype(jnp.float32))
    hub_place = pool_ref.shape[0] // TB - hub_count
    keyval_into(pool_ref, slice(hub_place * TB, None), hub_normed, w_qkv_ref, heads, head_dim)
    load.wait()
    group = max(head_dim, 128)
    for r in range(local):
        rows = slice(r * TB, (r + 1) * TB)
        places = []
        for t in range(tiles):
            col = cols_ref[head_here * local + r, t]
            near, block = col // per_group, col % per_group
            region = jnp.where(near == here, 0, jnp.where(near // 2 == here // 2, 1, 2))
            index = region * per_group + ((block // local) ^ head_here) * local + block % local
            index = jnp.where(col < hub_base, index, hub_place + col - hub_base)
            places.append(pl.ds(pl.multiple_of(index * TB, TB), TB))
        edges = jnp.concatenate([mask[r, t].astype(jnp.float32) for t in range(tiles)], axis=1)
        for g in range(width // group):
            cols = slice(g * group, (g + 1) * group)
            beyond = slice(width + g * group, width + (g + 1) * group)
            keys = jnp.concatenate([pool_ref[at, cols] for at in places], axis=0)
            values = jnp.concatenate([pool_ref[at, beyond] for at in places], axis=0)
            attn[rows, cols] = attention(query_ref[rows, cols], keys, values, edges, head_dim)
    mid = tokens_ref[...].astype(jnp.float32) + jnp.dot(
        attn[...], w_out_ref[...], preferred_element_type=jnp.float32
    )
    normed = layer_norm(mid)
    up = jnp.dot(normed, w_up_ref[...], preferred_element_type=jnp.float32)
    hidden = (0.5 * up * (1.0 + lax.erf(up * (0.5**0.5)))).astype(jnp.bfloat16)
    out_ref[...] = (
        mid + jnp.dot(hidden, w_down_ref[...], preferred_element_type=jnp.float32)
    ).astype(jnp.bfloat16)


def attention(query, keys, values, edges, head_dim):
    per = query.shape[1] // head_dim
    scale = 1.0 / head_dim**0.5
    lane = lax.broadcasted_iota(jnp.int32, query.shape, 1)
    result = None
    for s in range(per):
        here = (lane >= s * head_dim) & (lane < (s + 1) * head_dim)
        own = query if per == 1 else jnp.where(here, query.astype(jnp.float32), 0.0).astype(jnp.bfloat16)
        score = lax.dot_general(own, keys, (((1,), (1,)), ((), ())), preferred_element_type=jnp.float32)
        weight = jnp.exp(score * scale) * edges
        total = jnp.sum(weight, axis=1, keepdims=True)
        summed = jnp.dot(weight.astype(jnp.bfloat16), values, preferred_element_type=jnp.float32)
        one = summed / total
        result = one if result is None else jnp.where(here, one, result)
    return result.astype(jnp.bfloat16)


def finish(cols, tokens, query, mask, w_qkv, w_out, w_up, w_down, around, pool, heads, head_dim, hub_count, hub_base):
    node_dev, width = tokens.shape
    bf16 = jnp.bfloat16
    return pl.pallas_call(
        functools.partial(finish_kernel, heads, head_dim, hub_count, hub_base),
        out_shape=[jax.ShapeDtypeStruct(tokens.shape, bf16), jax.ShapeDtypeStruct(pool.shape, bf16)],
        in_specs=[pl.BlockSpec(memory_space=pltpu.SMEM)]
        + [VMEM] * 2
        + [pl.BlockSpec(memory_space=pltpu.HBM)]
        + [VMEM] * 7,
        out_specs=[VMEM, VMEM],
        input_output_aliases={10: 1},
        scratch_shapes=[
            pltpu.VMEM((hub_count * TB, width), bf16),
            pltpu.VMEM((node_dev // TB,) + mask.shape[1:], jnp.int32),
            pltpu.VMEM((node_dev, width), bf16),
            pltpu.SemaphoreType.DMA,
        ],
        compiler_params=pltpu.CompilerParams(vmem_limit_bytes=20 << 20),
        name="finish",
    )(cols, tokens, query, mask, w_qkv, w_out, w_up, w_down, *around, pool)[0]


def body(tokens, w_qkv, w_out, w_up, w_down, tile_cols, tile_mask, hub_blocks):
    node_dev, width = tokens.shape
    nodes = lax.axis_size("nodes")
    heads = lax.axis_size("heads")
    head_dim = width // heads
    per_group = tile_cols.shape[0]
    hub_count = hub_blocks.shape[0]
    local = node_dev // TB
    in_row = heads // 4
    areas = nodes // 2 * in_row
    go = functools.partial(send, nodes=nodes, heads=heads)

    def core(value):
        return go(value, where=lambda n, h: (n, h ^ 1))

    def pair(value):
        return go(value, where=lambda n, h: (n ^ 1, h))

    def across(value):
        return go(value, where=lambda n, h: (n ^ 1, h ^ 2))

    def side(value, offset=2):
        return go(value, where=lambda n, h: (n, h ^ offset))

    def along(value, by=1):
        return go(value, where=lambda n, h: (n + (2 - 4 * (n & 1)) * by, h))

    weights = w_qkv
    if head_dim % 128:
        weights = w_qkv.reshape(width, heads, 3, head_dim).swapaxes(1, 2).reshape(width, 3 * width)
    keyval = functools.partial(
        keyvals, w_qkv=weights, heads=heads, head_dim=head_dim, blocks=3 * per_group + hub_count
    )

    ring = areas == 4 and in_row == 1
    steps = [1]
    while steps[-1] * 4 < areas:
        steps.append(steps[-1] * 4)

    def reach(step):
        return [s * step for s in (1, 2, 3) if s * step < areas]

    def area_of(n, h):
        return n // 2 * in_row + h // 4

    def to_area(n, h, shift):
        at = area_of(n, h) ^ shift
        return at // in_row * 2 + n % 2, at % in_row * 4 + h % 4

    def owner(block):
        return block // per_group, block % per_group // local

    def picked_from(block, here, head_here):
        n, h = owner(block)
        offset = (n + here) % 2 * 4 + ((h % 4) ^ (head_here % 4))
        return offset * local + block % local

    def ring_from(block, here, head_here):
        ahead = area_of(here, head_here) + 4 - area_of(*owner(block))
        return jnp.where(here % 2 == 0, ahead, 8 - ahead) % 4

    def area_from(step):
        return lambda block, here, head_here: (area_of(*owner(block)) ^ area_of(here, head_here)) // step % 4

    whence = (picked_from, ring_from) if ring else (picked_from, *map(area_from, steps))

    other = range(2, heads, 2)
    sides = [side(tokens, o) for o in other]
    paired = pair(tokens)
    here, head_here = place()
    strip_at = ((1 - here % 2) * 4 + ((head_here % 4) ^ 2) // 2 * 2) * PIECE
    strip = lax.dynamic_slice_in_dim(tokens.reshape(local, TB, width), strip_at, 2 * PIECE, 1)
    strip = across(strip.reshape(local * 2 * PIECE, width))
    token_core = core(tokens)
    pool, query, again, codes = keyval(None, 0, tokens, token_core, hub_blocks=hub_blocks, whence=whence)
    paired, strip, pool, query, codes, *sides = lax.optimization_barrier((paired, strip, pool, query, codes, *sides))

    far = along(paired)

    paired_core, strip_core = core(paired), core(strip)
    sides_core = [core(v) for v in sides]
    paired_sides = [side(paired, o) for o in other]
    sources = [again, token_core, sides[0], sides_core[0], paired, paired_core, strip, strip_core]
    piece = pick_pieces(codes, sources)

    for k, (value, other_value) in enumerate(zip(sides, sides_core)):
        pool = keyval(pool, 2 + 2 * k, value, other_value, after=(piece,))
    far, pool = lax.optimization_barrier((far, pool))
    far_sides = [side(far, o) for o in other]
    far_core = core(far)
    pool = keyval(pool, heads, paired, paired_core)

    if ring:
        got = [piece, along(piece), along(piece, 2), along(piece, -1)]
        got, pool, paired_sides = lax.optimization_barrier((got, pool, paired_sides))
        piece = choose_pieces(codes, 1, got)
    else:
        for i, step in enumerate(steps):
            got = [go(piece, where=lambda n, h, s=s: to_area(n, h, s)) for s in reach(step)]
            piece = choose_pieces(codes, 1 + i, [piece, *got])

    around = [piece, side(piece), pair(piece), across(piece)]
    paired_sides_core = [core(v) for v in paired_sides]
    far_sides_core = [core(v) for v in far_sides]
    for k, (value, other_value) in enumerate(zip(paired_sides, paired_sides_core)):
        pool = keyval(pool, heads + 2 + 2 * k, value, other_value)
    for k, (value, other_value) in enumerate(zip([far, *far_sides], [far_core, *far_sides_core])):
        pool = keyval(pool, 2 * heads + 2 * k, value, other_value)
    around, pool = lax.optimization_barrier((around, pool))

    around = jnp.concatenate(around, axis=0)
    around = [around, core(around)]
    return finish(
        tile_cols, tokens, query, tile_mask, weights, w_out, w_up, w_down, around, pool, heads, head_dim, hub_count, per_group * nodes
    )


def solution(mesh):
    placed = (
        P(("nodes", "heads"), None),
        P(),
        P(),
        P(),
        P(),
        P("nodes", None),
        P("nodes", None, None, None),
        P(),
    )
    return jax.shard_map(
        body, mesh=mesh, in_specs=placed, out_specs=P(("nodes", "heads"), None), check_vma=False
    )
```

```python
import functools

import jax
import jax.numpy as jnp
from jax import lax
from jax.experimental import pallas as pl
from jax.experimental.pallas import tpu as pltpu
from jax.sharding import PartitionSpec as P

TB = 128
PIECES = 8
PIECE = TB // PIECES
AXES = ("nodes", "heads")
ANY = pl.BlockSpec(memory_space=pl.ANY)
VMEM = pl.BlockSpec(memory_space=pltpu.VMEM)


def send(value, nodes, heads, where):
    pairs = []
    for n in range(nodes):
        for h in range(heads):
            to_n, to_h = where(n, h)
            pairs.append((n * heads + h, to_n % nodes * heads + to_h))
    return lax.ppermute(value, AXES, pairs)


def layer_norm(value_rows):
    mean = jnp.mean(value_rows, axis=-1, keepdims=True)
    centered = value_rows - mean
    spread = jnp.mean(centered * centered, axis=-1, keepdims=True)
    return (centered * lax.rsqrt(spread + 1e-05)).astype(jnp.bfloat16)


def project(normed, w_ref, cols):
    return jnp.dot(normed, w_ref[:, cols], preferred_element_type=jnp.float32).astype(
        jnp.bfloat16
    )


def keyval_into(out_ref, rows, normed, w_ref, heads, head_dim):
    width = heads * head_dim
    if head_dim % 128 == 0:
        for h in range(heads):
            both = project(normed, w_ref, slice((3 * h + 1) * head_dim, (3 * h + 3) * head_dim))
            out_ref[rows, h * head_dim : (h + 1) * head_dim] = both[:, :head_dim]
            out_ref[rows, width + h * head_dim : width + (h + 1) * head_dim] = both[:, head_dim:]
    else:
        out_ref[rows, :] = project(normed, w_ref, slice(width, 3 * width))


def query_into(out_ref, normed, w_ref, heads, head_dim):
    if head_dim % 128 == 0:
        for h in range(heads):
            out_ref[:, h * head_dim : (h + 1) * head_dim] = project(
                normed, w_ref, slice(3 * h * head_dim, (3 * h + 1) * head_dim)
            )
    else:
        out_ref[...] = project(normed, w_ref, slice(0, heads * head_dim))


def keyval_kernel(heads, head_dim, at, whence, first_ref, second_ref, w_ref, *refs):
    node_dev = first_ref.shape[0]
    pool_ref = refs[-1] if at else refs[-4]
    if not at:
        hubs_ref, codes_ref = refs[0], refs[-1]
        here, head_here = place()
        for j in range(hubs_ref.shape[0]):
            for i, code in enumerate(whence):
                number = code(hubs_ref[j], here, head_here).astype(jnp.float32)
                codes_ref[i, j * PIECE : (j + 1) * PIECE, :] = jnp.full((PIECE, 128), number)
    for k, ref in enumerate((first_ref, second_ref)):
        normed = layer_norm(ref[...].astype(jnp.float32))
        rows = slice((at + k) * node_dev, (at + k + 1) * node_dev)
        keyval_into(pool_ref, rows, normed, w_ref, heads, head_dim)
        if not at and not k:
            query_into(refs[-3], normed, w_ref, heads, head_dim)
            refs[-2][...] = ref[...]


def keyvals(pool, at, first, second, w_qkv, heads, head_dim, blocks, after=(), hub_blocks=None, whence=()):
    node_dev, width = first.shape
    out_shape = [jax.ShapeDtypeStruct((blocks * TB, 2 * width), jnp.bfloat16)]
    if not at:
        out_shape += [jax.ShapeDtypeStruct((node_dev, width), jnp.bfloat16)] * 2
        shape = (len(whence), hub_blocks.shape[0] * PIECE, 128)
        out_shape.append(jax.ShapeDtypeStruct(shape, jnp.float32))
    operands = [first, second, w_qkv, *after] + ([pool] if at else [hub_blocks])
    result = pl.pallas_call(
        functools.partial(keyval_kernel, heads, head_dim, at, whence),
        out_shape=out_shape,
        in_specs=[VMEM] * 3 + [ANY] * len(after) + [VMEM if at else pl.BlockSpec(memory_space=pltpu.SMEM)],
        out_specs=[VMEM] * len(out_shape),
        input_output_aliases={len(operands) - 1: 0} if at else {},
        compiler_params=pltpu.CompilerParams(vmem_limit_bytes=8 << 20),
        cost_estimate=pl.CostEstimate(
            flops=64 * node_dev * width * width, bytes_accessed=6 * width * width, transcendentals=0
        ),
        name="keyvals",
    )(*operands)
    return result if not at else result[0]


def later(value, *first):
    return lax.optimization_barrier((value, *first))[0]


def place():
    return lax.axis_index("nodes"), lax.axis_index("heads")


def chosen(code_ref, at, rows, candidates):
    width = candidates[0].shape[1]
    code = jnp.concatenate([code_ref[at, rows, :]] * (width // 128), axis=1)
    result = candidates[0].astype(jnp.float32)
    for k, value in enumerate(candidates[1:], 1):
        result = jnp.where(code == k, value.astype(jnp.float32), result)
    return result.astype(jnp.bfloat16)


def pick_kernel(hub_count, local, code_ref, *refs):
    *sources, mine_ref, theirs_ref = refs
    here, head_here = place()
    lane = head_here % 2
    for out_ref, core in ((mine_ref, lane), (theirs_ref, 1 - lane)):
        piece = here % 2 * 4 + head_here % 4 - lane + core
        candidates = []
        for k, ref in enumerate(sources):
            for slot in range(local):
                row = slot * TB + piece * PIECE if k < 3 else (slot * 2 + core) * PIECE
                candidates.append(ref[pl.ds(pl.multiple_of(row, PIECE), PIECE), :])
        for j in range(hub_count):
            rows = slice(j * PIECE, (j + 1) * PIECE)
            out_ref[rows, :] = chosen(code_ref, 0, rows, candidates)


def pick_pieces(codes, sources):
    node_dev, width = sources[0].shape
    rows = codes.shape[1]
    return pl.pallas_call(
        functools.partial(pick_kernel, rows // PIECE, node_dev // TB),
        out_shape=[jax.ShapeDtypeStruct((rows, width), jnp.bfloat16)] * 2,
        in_specs=[VMEM] * (1 + len(sources)),
        out_specs=[VMEM] * 2,
        compiler_params=pltpu.CompilerParams(vmem_limit_bytes=4 << 20),
        name="pick_pieces",
    )(codes, *sources)


def choose_kernel(at, code_ref, *refs):
    *sources, piece_ref = refs
    piece_ref[...] = chosen(code_ref, at, slice(None), [ref[...] for ref in sources])


def choose_pieces(codes, at, sources):
    return pl.pallas_call(
        functools.partial(choose_kernel, at),
        out_shape=jax.ShapeDtypeStruct(sources[0].shape, jnp.bfloat16),
        in_specs=[VMEM] * (1 + len(sources)),
        out_specs=VMEM,
        compiler_params=pltpu.CompilerParams(vmem_limit_bytes=4 << 20),
        name="choose_pieces",
    )(codes, *sources)


def hub_keyval_into(pool_ref, scratch, rows_ref, lane, w_ref, heads, head_dim, hub_count):
    here, head_here = place()
    mine = here % 2 * 4 + head_here % 4
    keyval_into(scratch, slice(None), layer_norm(rows_ref[...].astype(jnp.float32)), w_ref, heads, head_dim)
    hub_place = pool_ref.shape[0] - hub_count * TB
    for k in range(PIECES // 2):
        for j in range(hub_count):
            row = (k * hub_count + j) * PIECE
            at = hub_place + j * TB + (mine ^ (2 * k + lane)) * PIECE
            pool_ref[pl.ds(pl.multiple_of(at, PIECE), PIECE), :] = scratch[row : row + PIECE, :]


def hub_half_kernel(heads, head_dim, hub_count, rows_ref, w_ref, _, pool_ref, scratch):
    hub_keyval_into(pool_ref, scratch, rows_ref, 0, w_ref, heads, head_dim, hub_count)


def hub_half(pool, rows, w_qkv, heads, head_dim, hub_count):
    return pl.pallas_call(
        functools.partial(hub_half_kernel, heads, head_dim, hub_count),
        out_shape=jax.ShapeDtypeStruct(pool.shape, pool.dtype),
        in_specs=[VMEM] * 3,
        out_specs=VMEM,
        input_output_aliases={2: 0},
        scratch_shapes=[pltpu.VMEM((rows.shape[0], pool.shape[1]), pool.dtype)],
        compiler_params=pltpu.CompilerParams(vmem_limit_bytes=8 << 20),
        name="hub_half",
    )(rows, w_qkv, pool)


def finish_kernel(
    heads, head_dim, hub_count, hub_base, plan_ref,
    tokens_ref, query_ref, mask, w_qkv_ref, w_out_ref, w_up_ref, w_down_ref, *refs
):
    around_ref, _, out_ref, pool_ref, hub_keyvals, attn, cols_ref, sem = refs
    node_dev, width = tokens_ref.shape
    local = node_dev // TB
    per_group, tiles = plan_ref.shape
    here, head_here = place()
    load = pltpu.make_async_copy(plan_ref, cols_ref, sem)
    load.start()
    hub_keyval_into(pool_ref, hub_keyvals, around_ref, 1, w_qkv_ref, heads, head_dim, hub_count)
    hub_place = pool_ref.shape[0] // TB - hub_count
    load.wait()
    group = max(head_dim, 128)
    for r in range(local):
        rows = slice(r * TB, (r + 1) * TB)
        places = []
        for t in range(tiles):
            col = cols_ref[head_here * local + r, t]
            near, block = col // per_group, col % per_group
            region = jnp.where(near == here, 0, jnp.where(near // 2 == here // 2, 1, 2))
            index = region * per_group + ((block // local) ^ head_here) * local + block % local
            index = jnp.where(col < hub_base, index, hub_place + col - hub_base)
            places.append(pl.ds(pl.multiple_of(index * TB, TB), TB))
        edges = jnp.concatenate([mask[r, t].astype(jnp.float32) for t in range(tiles)], axis=1)
        for g in range(width // group):
            cols = slice(g * group, (g + 1) * group)
            beyond = slice(width + g * group, width + (g + 1) * group)
            keys = jnp.concatenate([pool_ref[at, cols] for at in places], axis=0)
            values = jnp.concatenate([pool_ref[at, beyond] for at in places], axis=0)
            attn[rows, cols] = attention(query_ref[rows, cols], keys, values, edges, head_dim)
    mid = tokens_ref[...].astype(jnp.float32) + jnp.dot(
        attn[...], w_out_ref[...], preferred_element_type=jnp.float32
    )
    normed = layer_norm(mid)
    up = jnp.dot(normed, w_up_ref[...], preferred_element_type=jnp.float32)
    hidden = (0.5 * up * (1.0 + lax.erf(up * (0.5**0.5)))).astype(jnp.bfloat16)
    out_ref[...] = (
        mid + jnp.dot(hidden, w_down_ref[...], preferred_element_type=jnp.float32)
    ).astype(jnp.bfloat16)


def attention(query, keys, values, edges, head_dim):
    per = query.shape[1] // head_dim
    scale = 1.0 / head_dim**0.5
    lane = lax.broadcasted_iota(jnp.int32, query.shape, 1)
    result = None
    for s in range(per):
        here = (lane >= s * head_dim) & (lane < (s + 1) * head_dim)
        own = query if per == 1 else jnp.where(here, query.astype(jnp.float32), 0.0).astype(jnp.bfloat16)
        score = lax.dot_general(own, keys, (((1,), (1,)), ((), ())), preferred_element_type=jnp.float32)
        weight = jnp.exp(score * scale) * edges
        total = jnp.sum(weight, axis=1, keepdims=True)
        summed = jnp.dot(weight.astype(jnp.bfloat16), values, preferred_element_type=jnp.float32)
        one = summed / total
        result = one if result is None else jnp.where(here, one, result)
    return result.astype(jnp.bfloat16)


def finish(cols, tokens, query, mask, w_qkv, w_out, w_up, w_down, around, pool, heads, head_dim, hub_count, hub_base):
    node_dev, width = tokens.shape
    bf16 = jnp.bfloat16
    return pl.pallas_call(
        functools.partial(finish_kernel, heads, head_dim, hub_count, hub_base),
        out_shape=[jax.ShapeDtypeStruct(tokens.shape, bf16), jax.ShapeDtypeStruct(pool.shape, bf16)],
        in_specs=[ANY] + [VMEM] * 9,
        out_specs=[VMEM, VMEM],
        input_output_aliases={9: 1},
        scratch_shapes=[
            pltpu.VMEM((around.shape[0], 2 * width), bf16),
            pltpu.VMEM((node_dev, width), bf16),
            pltpu.SMEM(cols.shape, jnp.int32),
            pltpu.SemaphoreType.DMA,
        ],
        compiler_params=pltpu.CompilerParams(vmem_limit_bytes=20 << 20),
        name="finish",
    )(cols, tokens, query, mask, w_qkv, w_out, w_up, w_down, around, pool)[0]


def body(tokens, w_qkv, w_out, w_up, w_down, tile_cols, tile_mask, hub_blocks):
    node_dev, width = tokens.shape
    nodes = lax.axis_size("nodes")
    heads = lax.axis_size("heads")
    head_dim = width // heads
    per_group = tile_cols.shape[0]
    hub_count = hub_blocks.shape[0]
    local = node_dev // TB
    in_row = heads // 4
    areas = nodes // 2 * in_row
    go = functools.partial(send, nodes=nodes, heads=heads)

    def core(value):
        return go(value, where=lambda n, h: (n, h ^ 1))

    def pair(value):
        return go(value, where=lambda n, h: (n ^ 1, h))

    def across(value):
        return go(value, where=lambda n, h: (n ^ 1, h ^ 2))

    def side(value, offset=2):
        return go(value, where=lambda n, h: (n, h ^ offset))

    def along(value, by=1):
        return go(value, where=lambda n, h: (n + (2 - 4 * (n & 1)) * by, h))

    weights = w_qkv
    if head_dim % 128:
        weights = w_qkv.reshape(width, heads, 3, head_dim).swapaxes(1, 2).reshape(width, 3 * width)
    keyval = functools.partial(
        keyvals, w_qkv=weights, heads=heads, head_dim=head_dim, blocks=3 * per_group + hub_count
    )

    ring = areas == 4 and in_row == 1
    steps = [1]
    while steps[-1] * 4 < areas:
        steps.append(steps[-1] * 4)

    def reach(step):
        return [s * step for s in (1, 2, 3) if s * step < areas]

    def area_of(n, h):
        return n // 2 * in_row + h // 4

    def to_area(n, h, shift):
        at = area_of(n, h) ^ shift
        return at // in_row * 2 + n % 2, at % in_row * 4 + h % 4

    def owner(block):
        return block // per_group, block % per_group // local

    def picked_from(block, here, head_here):
        n, h = owner(block)
        offset = (n + here) % 2 * 2 + (h // 2 + head_here // 2) % 2
        return offset * local + block % local

    def lane_from(block, here, head_here):
        return (owner(block)[1] + head_here) % 2

    def ring_from(block, here, head_here):
        ahead = area_of(here, head_here) + 4 - area_of(*owner(block))
        return jnp.where(here % 2 == 0, ahead, 8 - ahead) % 4

    def area_from(step):
        return lambda block, here, head_here: (area_of(*owner(block)) ^ area_of(here, head_here)) // step % 4

    whence = (picked_from, lane_from, *([ring_from] if ring else map(area_from, steps)))

    other = range(2, heads, 2)
    sides = [side(tokens, o) for o in other]
    paired = pair(tokens)
    here, head_here = place()
    strip_at = ((1 - here % 2) * 4 + ((head_here % 4) ^ 2) // 2 * 2) * PIECE
    strip = lax.dynamic_slice_in_dim(tokens.reshape(local, TB, width), strip_at, 2 * PIECE, 1)
    strip = across(strip.reshape(local * 2 * PIECE, width))
    token_core = core(tokens)
    pool, query, again, codes = keyval(None, 0, tokens, token_core, hub_blocks=hub_blocks, whence=whence)
    far = along(paired)
    edges = lax.dynamic_slice_in_dim(tile_mask, head_here * local, local, 0)
    paired, strip, pool, query, codes, edges, *sides = lax.optimization_barrier(
        (paired, strip, pool, query, codes, edges, *sides)
    )


    mine, theirs = pick_pieces(codes, [again, sides[0], paired, strip])
    paired_core = core(paired)
    sides_core = [core(v) for v in sides]
    theirs = later(core(theirs), paired_core, *sides_core)
    piece = choose_pieces(codes, 1, [mine, theirs])
    paired_sides = [pair(later(v, theirs)) for v in sides]

    pool = keyval(pool, heads, paired, paired_core, after=(piece,))
    far, pool = lax.optimization_barrier((far, pool))
    far_sides = [side(far, o) for o in other]
    for k, (value, other_value) in enumerate(zip(sides, sides_core)):
        pool = keyval(pool, 2 + 2 * k, value, other_value, after=(far,))
    paired_core2 = [core(later(v, far)) for v in paired_sides]

    if ring:
        got = [piece, along(piece), along(piece, 2), along(piece, -1)]
        got, pool, paired_sides = lax.optimization_barrier((got, pool, paired_sides))
        piece = choose_pieces(codes, 2, got)
    else:
        for i, step in enumerate(steps):
            got = [go(piece, where=lambda n, h, s=s: to_area(n, h, s)) for s in reach(step)]
            piece = choose_pieces(codes, 2 + i, [piece, *got])

    around = [piece, side(piece), pair(piece), across(piece)]
    for k, (value, other_value) in enumerate(zip(paired_sides, paired_core2)):
        pool = keyval(pool, heads + 2 + 2 * k, value, other_value)
    for k, value in enumerate([far, *far_sides]):
        pool = keyval(pool, 2 * heads + 2 * k, value, core(later(value, piece)))
    around, pool = lax.optimization_barrier((around, pool))

    around = jnp.concatenate(around, axis=0)
    pool = hub_half(pool, around, weights, heads, head_dim, hub_count)
    around = core(around)
    return finish(
        tile_cols, again, query, edges, weights, w_out, w_up, w_down, around, pool, heads, head_dim, hub_count, per_group * nodes
    )


def solution(mesh):
    placed = (
        P(("nodes", "heads"), None),
        P(),
        P(),
        P(),
        P(),
        P("nodes", None),
        P("nodes", None, None, None),
        P(),
    )
    return jax.shard_map(
        body, mesh=mesh, in_specs=placed, out_specs=P(("nodes", "heads"), None), check_vma=False
    )
```

```python
import functools

import jax
import jax.numpy as jnp
from jax import lax
from jax.experimental import pallas as pl
from jax.experimental.pallas import tpu as pltpu
from jax.sharding import PartitionSpec as P

TB = 128
PIECES = 8
PIECE = TB // PIECES
AXES = ("nodes", "heads")
ANY = pl.BlockSpec(memory_space=pl.ANY)
VMEM = pl.BlockSpec(memory_space=pltpu.VMEM)


def send(value, nodes, heads, where):
    pairs = []
    for n in range(nodes):
        for h in range(heads):
            to_n, to_h = where(n, h)
            pairs.append((n * heads + h, to_n % nodes * heads + to_h))
    return lax.ppermute(value, AXES, pairs)


def layer_norm(value_rows):
    mean = jnp.mean(value_rows, axis=-1, keepdims=True)
    centered = value_rows - mean
    spread = jnp.mean(centered * centered, axis=-1, keepdims=True)
    return (centered * lax.rsqrt(spread + 1e-05)).astype(jnp.bfloat16)


def project(normed, w_ref, cols):
    return jnp.dot(normed, w_ref[:, cols], preferred_element_type=jnp.float32).astype(
        jnp.bfloat16
    )


def keyval_into(out_ref, rows, normed, w_ref, heads, head_dim):
    width = heads * head_dim
    if head_dim % 128 == 0:
        for h in range(heads):
            both = project(normed, w_ref, slice((3 * h + 1) * head_dim, (3 * h + 3) * head_dim))
            out_ref[rows, h * head_dim : (h + 1) * head_dim] = both[:, :head_dim]
            out_ref[rows, width + h * head_dim : width + (h + 1) * head_dim] = both[:, head_dim:]
    else:
        out_ref[rows, :] = project(normed, w_ref, slice(width, 3 * width))


def query_into(out_ref, normed, w_ref, heads, head_dim):
    if head_dim % 128 == 0:
        for h in range(heads):
            out_ref[:, h * head_dim : (h + 1) * head_dim] = project(
                normed, w_ref, slice(3 * h * head_dim, (3 * h + 1) * head_dim)
            )
    else:
        out_ref[...] = project(normed, w_ref, slice(0, heads * head_dim))


def keyval_kernel(heads, head_dim, at, whence, first_ref, second_ref, w_ref, *refs):
    node_dev = first_ref.shape[0]
    pool_ref = refs[-1] if at else refs[-4]
    if not at:
        hubs_ref, codes_ref = refs[0], refs[-1]
        here, head_here = place()
        for j in range(hubs_ref.shape[0]):
            for i, code in enumerate(whence):
                number = code(hubs_ref[j], here, head_here).astype(jnp.float32)
                codes_ref[i, j * PIECE : (j + 1) * PIECE, :] = jnp.full((PIECE, 128), number)
    for k, ref in enumerate((first_ref, second_ref)):
        normed = layer_norm(ref[...].astype(jnp.float32))
        rows = slice((at + k) * node_dev, (at + k + 1) * node_dev)
        keyval_into(pool_ref, rows, normed, w_ref, heads, head_dim)
        if not at and not k:
            query_into(refs[-3], normed, w_ref, heads, head_dim)
            refs[-2][...] = ref[...]


def keyvals(pool, at, first, second, w_qkv, heads, head_dim, blocks, after=(), hub_blocks=None, whence=()):
    node_dev, width = first.shape
    out_shape = [jax.ShapeDtypeStruct((blocks * TB, 2 * width), jnp.bfloat16)]
    if not at:
        out_shape += [jax.ShapeDtypeStruct((node_dev, width), jnp.bfloat16)] * 2
        shape = (len(whence), hub_blocks.shape[0] * PIECE, 128)
        out_shape.append(jax.ShapeDtypeStruct(shape, jnp.float32))
    operands = [first, second, w_qkv, *after] + ([pool] if at else [hub_blocks])
    result = pl.pallas_call(
        functools.partial(keyval_kernel, heads, head_dim, at, whence),
        out_shape=out_shape,
        in_specs=[VMEM] * 3 + [ANY] * len(after) + [VMEM if at else pl.BlockSpec(memory_space=pltpu.SMEM)],
        out_specs=[VMEM] * len(out_shape),
        input_output_aliases={len(operands) - 1: 0} if at else {},
        compiler_params=pltpu.CompilerParams(vmem_limit_bytes=8 << 20),
        cost_estimate=pl.CostEstimate(
            flops=64 * node_dev * width * width, bytes_accessed=6 * width * width, transcendentals=0
        ),
        name="keyvals",
    )(*operands)
    return result if not at else result[0]


def later(value, *first):
    return lax.optimization_barrier((value, *first))[0]


def place():
    return lax.axis_index("nodes"), lax.axis_index("heads")


def chosen(code_ref, at, rows, candidates):
    width = candidates[0].shape[1]
    code = jnp.concatenate([code_ref[at, rows, :]] * (width // 128), axis=1)
    result = candidates[0].astype(jnp.float32)
    for k, value in enumerate(candidates[1:], 1):
        result = jnp.where(code == k, value.astype(jnp.float32), result)
    return result.astype(jnp.bfloat16)


def pick_kernel(hub_count, local, code_ref, *refs):
    *sources, mine_ref, theirs_ref = refs
    here, head_here = place()
    lane = head_here % 2
    for out_ref, core in ((mine_ref, lane), (theirs_ref, 1 - lane)):
        piece = here % 2 * 4 + head_here % 4 - lane + core
        candidates = []
        for k, ref in enumerate(sources):
            for slot in range(local):
                row = slot * TB + piece * PIECE if k < 3 else (slot * 2 + core) * PIECE
                candidates.append(ref[pl.ds(pl.multiple_of(row, PIECE), PIECE), :])
        for j in range(hub_count):
            rows = slice(j * PIECE, (j + 1) * PIECE)
            out_ref[rows, :] = chosen(code_ref, 0, rows, candidates)


def pick_pieces(codes, sources):
    node_dev, width = sources[0].shape
    rows = codes.shape[1]
    return pl.pallas_call(
        functools.partial(pick_kernel, rows // PIECE, node_dev // TB),
        out_shape=[jax.ShapeDtypeStruct((rows, width), jnp.bfloat16)] * 2,
        in_specs=[VMEM] * (1 + len(sources)),
        out_specs=[VMEM] * 2,
        compiler_params=pltpu.CompilerParams(vmem_limit_bytes=4 << 20),
        name="pick_pieces",
    )(codes, *sources)


def choose_kernel(at, code_ref, *refs):
    *sources, piece_ref = refs
    piece_ref[...] = chosen(code_ref, at, slice(None), [ref[...] for ref in sources])


def choose_pieces(codes, at, sources):
    return pl.pallas_call(
        functools.partial(choose_kernel, at),
        out_shape=jax.ShapeDtypeStruct(sources[0].shape, jnp.bfloat16),
        in_specs=[VMEM] * (1 + len(sources)),
        out_specs=VMEM,
        compiler_params=pltpu.CompilerParams(vmem_limit_bytes=4 << 20),
        name="choose_pieces",
    )(codes, *sources)


def hub_keyval_into(pool_ref, scratch, rows_ref, lane, w_ref, heads, head_dim, hub_count):
    here, head_here = place()
    mine = here % 2 * 4 + head_here % 4
    keyval_into(scratch, slice(None), layer_norm(rows_ref[...].astype(jnp.float32)), w_ref, heads, head_dim)
    hub_place = pool_ref.shape[0] - hub_count * TB
    for k in range(PIECES // 2):
        for j in range(hub_count):
            row = (k * hub_count + j) * PIECE
            at = hub_place + j * TB + (mine ^ (2 * k + lane)) * PIECE
            pool_ref[pl.ds(pl.multiple_of(at, PIECE), PIECE), :] = scratch[row : row + PIECE, :]


def hub_half_kernel(heads, head_dim, hub_count, rows_ref, w_ref, _, pool_ref, scratch):
    hub_keyval_into(pool_ref, scratch, rows_ref, 0, w_ref, heads, head_dim, hub_count)


def hub_half(pool, rows, w_qkv, heads, head_dim, hub_count):
    return pl.pallas_call(
        functools.partial(hub_half_kernel, heads, head_dim, hub_count),
        out_shape=jax.ShapeDtypeStruct(pool.shape, pool.dtype),
        in_specs=[VMEM] * 3,
        out_specs=VMEM,
        input_output_aliases={2: 0},
        scratch_shapes=[pltpu.VMEM((rows.shape[0], pool.shape[1]), pool.dtype)],
        compiler_params=pltpu.CompilerParams(vmem_limit_bytes=8 << 20),
        name="hub_half",
    )(rows, w_qkv, pool)


def finish_kernel(
    heads, head_dim, hub_count, hub_base, plan_ref,
    tokens_ref, query_ref, mask, w_qkv_ref, w_out_ref, w_up_ref, w_down_ref, *refs
):
    around_ref, _, out_ref, pool_ref, hub_keyvals, attn, cols_ref, sem = refs
    node_dev, width = tokens_ref.shape
    local = node_dev // TB
    per_group, tiles = plan_ref.shape
    here, head_here = place()
    load = pltpu.make_async_copy(plan_ref, cols_ref, sem)
    load.start()
    hub_keyval_into(pool_ref, hub_keyvals, around_ref, 1, w_qkv_ref, heads, head_dim, hub_count)
    hub_place = pool_ref.shape[0] // TB - hub_count
    load.wait()
    group = max(head_dim, 128)
    for r in range(local):
        rows = slice(r * TB, (r + 1) * TB)
        places = []
        for t in range(tiles):
            col = cols_ref[head_here * local + r, t]
            near, block = col // per_group, col % per_group
            region = jnp.where(near == here, 0, jnp.where(near // 2 == here // 2, 1, 2))
            index = region * per_group + ((block // local) ^ head_here) * local + block % local
            index = jnp.where(col < hub_base, index, hub_place + col - hub_base)
            places.append(pl.ds(pl.multiple_of(index * TB, TB), TB))
        edges = jnp.concatenate([mask[r, t] for t in range(tiles)], axis=1)
        for g in range(width // group):
            cols = slice(g * group, (g + 1) * group)
            beyond = slice(width + g * group, width + (g + 1) * group)
            keys = jnp.concatenate([pool_ref[at, cols] for at in places], axis=0)
            values = jnp.concatenate([pool_ref[at, beyond] for at in places], axis=0)
            attn[rows, cols] = attention(query_ref[rows, cols], keys, values, edges, head_dim)
    mid = tokens_ref[...].astype(jnp.float32) + jnp.dot(
        attn[...], w_out_ref[...], preferred_element_type=jnp.float32
    )
    normed = layer_norm(mid)
    up = jnp.dot(normed, w_up_ref[...], preferred_element_type=jnp.float32)
    hidden = (0.5 * up * (1.0 + lax.erf(up * (0.5**0.5)))).astype(jnp.bfloat16)
    out_ref[...] = (
        mid + jnp.dot(hidden, w_down_ref[...], preferred_element_type=jnp.float32)
    ).astype(jnp.bfloat16)


def attention(query, keys, values, edges, head_dim):
    per = query.shape[1] // head_dim
    scale = 1.0 / head_dim**0.5
    lane = lax.broadcasted_iota(jnp.int32, query.shape, 1)
    result = None
    for s in range(per):
        here = (lane >= s * head_dim) & (lane < (s + 1) * head_dim)
        own = query if per == 1 else jnp.where(here, query.astype(jnp.float32), 0.0).astype(jnp.bfloat16)
        score = lax.dot_general(own, keys, (((1,), (1,)), ((), ())), preferred_element_type=jnp.float32)
        weight = jnp.exp(score * scale) * edges
        total = jnp.sum(weight, axis=1, keepdims=True)
        summed = jnp.dot(weight.astype(jnp.bfloat16), values, preferred_element_type=jnp.float32)
        one = summed / total
        result = one if result is None else jnp.where(here, one, result)
    return result.astype(jnp.bfloat16)


def finish(cols, tokens, query, mask, w_qkv, w_out, w_up, w_down, around, pool, heads, head_dim, hub_count, hub_base):
    node_dev, width = tokens.shape
    bf16 = jnp.bfloat16
    return pl.pallas_call(
        functools.partial(finish_kernel, heads, head_dim, hub_count, hub_base),
        out_shape=[jax.ShapeDtypeStruct(tokens.shape, bf16), jax.ShapeDtypeStruct(pool.shape, bf16)],
        in_specs=[ANY] + [VMEM] * 9,
        out_specs=[VMEM, VMEM],
        input_output_aliases={9: 1},
        scratch_shapes=[
            pltpu.VMEM((around.shape[0], 2 * width), bf16),
            pltpu.VMEM((node_dev, width), bf16),
            pltpu.SMEM(cols.shape, jnp.int32),
            pltpu.SemaphoreType.DMA,
        ],
        compiler_params=pltpu.CompilerParams(vmem_limit_bytes=20 << 20),
        name="finish",
    )(cols, tokens, query, mask, w_qkv, w_out, w_up, w_down, around, pool)[0]


def body(tokens, w_qkv, w_out, w_up, w_down, tile_cols, tile_mask, hub_blocks):
    node_dev, width = tokens.shape
    nodes = lax.axis_size("nodes")
    heads = lax.axis_size("heads")
    head_dim = width // heads
    per_group = tile_cols.shape[0]
    hub_count = hub_blocks.shape[0]
    local = node_dev // TB
    in_row = heads // 4
    areas = nodes // 2 * in_row
    go = functools.partial(send, nodes=nodes, heads=heads)

    def core(value):
        return go(value, where=lambda n, h: (n, h ^ 1))

    def pair(value):
        return go(value, where=lambda n, h: (n ^ 1, h))

    def across(value):
        return go(value, where=lambda n, h: (n ^ 1, h ^ 2))

    def side(value, offset=2):
        return go(value, where=lambda n, h: (n, h ^ offset))

    def along(value, by=1):
        return go(value, where=lambda n, h: (n + (2 - 4 * (n & 1)) * by, h))

    weights = w_qkv
    if head_dim % 128:
        weights = w_qkv.reshape(width, heads, 3, head_dim).swapaxes(1, 2).reshape(width, 3 * width)
    keyval = functools.partial(
        keyvals, w_qkv=weights, heads=heads, head_dim=head_dim, blocks=3 * per_group + hub_count
    )

    ring = areas == 4 and in_row == 1
    steps = [1]
    while steps[-1] * 4 < areas:
        steps.append(steps[-1] * 4)

    def reach(step):
        return [s * step for s in (1, 2, 3) if s * step < areas]

    def area_of(n, h):
        return n // 2 * in_row + h // 4

    def to_area(n, h, shift):
        at = area_of(n, h) ^ shift
        return at // in_row * 2 + n % 2, at % in_row * 4 + h % 4

    def owner(block):
        return block // per_group, block % per_group // local

    def picked_from(block, here, head_here):
        n, h = owner(block)
        offset = (n + here) % 2 * 2 + (h // 2 + head_here // 2) % 2
        return offset * local + block % local

    def lane_from(block, here, head_here):
        return (owner(block)[1] + head_here) % 2

    def ring_from(block, here, head_here):
        ahead = area_of(here, head_here) + 4 - area_of(*owner(block))
        return jnp.where(here % 2 == 0, ahead, 8 - ahead) % 4

    def area_from(step):
        return lambda block, here, head_here: (area_of(*owner(block)) ^ area_of(here, head_here)) // step % 4

    whence = (picked_from, lane_from, *([ring_from] if ring else map(area_from, steps)))

    other = range(2, heads, 2)
    sides = [side(tokens, o) for o in other]
    paired = pair(tokens)
    here, head_here = place()
    strip_at = ((1 - here % 2) * 4 + ((head_here % 4) ^ 2) // 2 * 2) * PIECE
    strip = lax.dynamic_slice_in_dim(tokens.reshape(local, TB, width), strip_at, 2 * PIECE, 1)
    strip = across(strip.reshape(local * 2 * PIECE, width))
    token_core = core(tokens)
    pool, query, again, codes = keyval(None, 0, tokens, token_core, hub_blocks=hub_blocks, whence=whence)
    far = along(paired)
    edges = lax.dynamic_slice_in_dim(tile_mask, head_here * local, local, 0).astype(jnp.float32)
    paired, strip, pool, query, codes, edges, *sides = lax.optimization_barrier(
        (paired, strip, pool, query, codes, edges, *sides)
    )


    mine, theirs = pick_pieces(codes, [again, sides[0], paired, strip])
    paired_core = core(paired)
    sides_core = [core(v) for v in sides]
    theirs = later(core(theirs), paired_core, *sides_core)
    piece = choose_pieces(codes, 1, [mine, theirs])
    paired_sides = [pair(later(v, theirs)) for v in sides]

    pool = keyval(pool, heads, paired, paired_core, after=(piece,))
    far, pool = lax.optimization_barrier((far, pool))
    far_sides = [side(far, o) for o in other]
    for k, (value, other_value) in enumerate(zip(sides, sides_core)):
        pool = keyval(pool, 2 + 2 * k, value, other_value, after=(far,))
    paired_core2 = [core(later(v, far)) for v in paired_sides]

    if ring:
        got = [piece, along(piece), along(piece, 2), along(piece, -1)]
        got, pool, paired_sides = lax.optimization_barrier((got, pool, paired_sides))
        piece = choose_pieces(codes, 2, got)
    else:
        for i, step in enumerate(steps):
            got = [go(piece, where=lambda n, h, s=s: to_area(n, h, s)) for s in reach(step)]
            piece = choose_pieces(codes, 2 + i, [piece, *got])

    around = [piece, side(piece), pair(piece), across(piece)]
    for k, (value, other_value) in enumerate(zip(paired_sides, paired_core2)):
        pool = keyval(pool, heads + 2 + 2 * k, value, other_value)
    for k, value in enumerate([far, *far_sides]):
        pool = keyval(pool, 2 * heads + 2 * k, value, core(later(value, piece)))
    around, pool = lax.optimization_barrier((around, pool))

    around = jnp.concatenate(around, axis=0)
    pool = hub_half(pool, around, weights, heads, head_dim, hub_count)
    around = core(around)
    return finish(
        tile_cols, again, query, edges, weights, w_out, w_up, w_down, around, pool, heads, head_dim, hub_count, per_group * nodes
    )


def solution(mesh):
    placed = (
        P(("nodes", "heads"), None),
        P(),
        P(),
        P(),
        P(),
        P("nodes", None),
        P("nodes", None, None, None),
        P(),
    )
    return jax.shard_map(
        body, mesh=mesh, in_specs=placed, out_specs=P(("nodes", "heads"), None), check_vma=False
    )
```
